128 devices in a mesh: chan: 16 (over z, x_hi, core), sect: 8 (over x_lo, y).
Axes of the slice: x: 4 (x_hi: 2, x_lo: 2; x = x_hi * 2 + x_lo), y: 4, z: 4, core: 2. Of those that a mesh axis runs over, the one named last changes fastest.
Arguments:
- voltages: bfloat16 [2, 512, 524288], P(None, 'chan', 'sect'), may hold values from -6 to 6
- fir_taps: float32 [4, 4096], replicated, may hold values from -3 to 3
- station_map: int32 [512], replicated, may hold values from 0 to 511, each once
- band_start: int32 [32], replicated, may hold values from 0 to 4032, as said below
- calib: bfloat16 [2, 2048, 512], P(None, ('chan', 'sect')), may hold values from -6 to 6
- steer: bfloat16 [1024, 2, 512], P('sect'), may hold values from -0.1875 to 0.1875
- beam_index: int32 [500], replicated, may hold values from 0 to 1023
Outputs:
- visibility: float32 [2, 512, 512, 512], P(None, ('chan', 'sect'))
- beams: bfloat16 [2, 2048, 500, 128], P(None, ('chan', 'sect'))
The draws below stay inside these ranges and needn't reach their ends.
Inputs may be any that keep to these rules, and one draw needn't show every extreme that they name: `band_start`: distinct multiples of 64, so the kept sub-bands never share a channel.
All inputs are finite; a program needn't handle non-finite values.
Results may differ from the reference program's by a relative error of at most 0.02.
Values may be sent and summed in bfloat16 or wider, within the bound.
A program may use at most 192 MiB of HBM per device.

```python
import math
import jax
import jax.numpy as jnp
from jax import lax

STATIONS = 512
RADIX = 64
NFFT = 4096
TAPS = 4
FRAMES = 128
SAMPLES = 524288
AVG = 4
SUBW = 64
KEPT = 2048
VIS = 512
BEAMS = 500
ENTRIES = 1024


def draw_band_start(key, part):
    key = jax.random.fold_in(key, 11)
    slot_count = NFFT // SUBW
    band_count = KEPT // SUBW
    key_slots, key_order = jax.random.split(key)
    interior = jax.random.permutation(key_slots, slot_count - 2)[:band_count - 2] + 1
    chosen = jnp.concatenate([jnp.array([0, slot_count - 1], jnp.int32), interior.astype(jnp.int32)])
    shuffle = jax.random.permutation(key_order, band_count)
    return (chosen[shuffle] * SUBW).astype(jnp.int32)


def touch_ends(drawn, key, least, largest):
    dims = drawn.shape
    spot = [jax.random.randint(jax.random.fold_in(key, axis), (), 0, dims[axis]) for axis in range(len(dims))]
    drawn = drawn.at[tuple(spot)].set(least)
    longest = dims.index(max(dims))
    spot[longest] = (spot[longest] + 1) % dims[longest]
    return drawn.at[tuple(spot)].set(largest)


def level_of(stream_key, shape, cuts, low, top_value):
    loudness, own = 1.0, jax.random.fold_in(stream_key, 6)
    for position, shards_of in cuts:
        heights = jnp.exp(jax.random.uniform(jax.random.fold_in(own, position), (shards_of,), jnp.float32, low / len(cuts), top_value / len(cuts)))
        loudness = loudness * jnp.repeat(heights, shape[position] // shards_of).reshape([-1 if axis == position else 1 for axis in range(len(shape))])
    return loudness


def bell_draw(key, shape, deviation, bound, cuts=(), kind=jnp.bfloat16):
    values = jax.random.normal(key, shape, jnp.float32) * deviation
    if len(cuts) > 0:
        values = level_of(key, shape, cuts, -0.22, 0.18) * values
    return jnp.clip(values, min=-bound, max=bound).astype(kind)


def setup_inputs(seed: int = 0) -> dict:
    seeds = jax.random.split(jax.random.key(seed), 8)
    return {
        "voltages": bell_draw(seeds[0], (2, STATIONS, SAMPLES), 1.0, 6.0, ((1, 16), (2, 8))),
        "fir_taps": bell_draw(seeds[1], (TAPS, NFFT), 0.5, 3.0, (), jnp.float32),
        "station_map": jax.random.permutation(seeds[2], STATIONS).astype(jnp.int32),
        "band_start": draw_band_start(jax.random.fold_in(seeds[7], 71), 0),
        "calib": bell_draw(seeds[4], (2, KEPT, STATIONS), 1.0, 6.0, ((1, 128),)),
        "steer": bell_draw(seeds[5], (ENTRIES, 2, STATIONS), (2 * STATIONS) ** -0.5, 0.1875, ((0, 8),)),
        "beam_index": touch_ends(jax.random.randint(seeds[6], (BEAMS,), 0, ENTRIES), jax.random.fold_in(seeds[6], 1), 0, ENTRIES - 1).astype(jnp.int32),
    }


def reference(voltages, fir_taps, station_map, band_start, calib, steer, beam_index):
    inverse = jnp.zeros((STATIONS,), jnp.int32).at[station_map].set(jnp.arange(STATIONS, dtype=jnp.int32))
    kept_index = (band_start[:, None] + jnp.arange(SUBW, dtype=jnp.int32)[None, :]).reshape(-1)
    steps_idx = jnp.arange(RADIX, dtype=jnp.int32)
    twist_angle = (2.0 * math.pi / NFFT) * (steps_idx[:, None] * steps_idx[None, :]).astype(jnp.float32)
    twist = jnp.cos(twist_angle) - 1j * jnp.sin(twist_angle)

    def per_station(row):
        series = lax.dynamic_index_in_dim(voltages, row, 1, keepdims=False).astype(jnp.float32)
        padded = jnp.pad(series, ((0, 0), ((TAPS - 1) * NFFT, 0)))
        blocks = padded.reshape(2, FRAMES + TAPS - 1, NFFT)
        filtered = jnp.zeros((2, FRAMES, NFFT), jnp.float32)
        for tap_index in range(TAPS):
            filtered = filtered + fir_taps[tap_index][None, None, :] * blocks[:, TAPS - 1 - tap_index:TAPS - 1 - tap_index + FRAMES]
        rounded = lax.optimization_barrier(filtered.astype(jnp.bfloat16)).astype(jnp.float32)
        grid = (rounded[0] + 1j * rounded[1]).reshape(FRAMES, RADIX, RADIX)
        section = jnp.fft.fft(grid, axis=1, norm="ortho") * twist[None, :, :]
        section_parts = jnp.stack([section.real, section.imag]).astype(jnp.bfloat16)
        section_parts = lax.optimization_barrier(section_parts).astype(jnp.float32)
        second = jnp.fft.fft(section_parts[0] + 1j * section_parts[1], axis=2, norm="ortho")
        spectrum = jnp.transpose(second, (0, 2, 1)).reshape(FRAMES, NFFT)
        picked = jnp.stack([spectrum.real[:, kept_index], spectrum.imag[:, kept_index]])
        return jnp.transpose(picked, (0, 2, 1)).astype(jnp.bfloat16)

    spectra = lax.map(per_station, inverse)
    weights = steer[beam_index].astype(jnp.float32)
    scale = 1.0 / (AVG * FRAMES)

    def per_group(group):
        start = (group * AVG).astype(jnp.int32)
        piece = lax.dynamic_slice_in_dim(spectra, start, AVG, 2).astype(jnp.float32)
        swapped = jnp.stack([piece[:, 1], -piece[:, 0]], axis=1)
        real_vis = jnp.einsum('pcaf,qcaf->pq', piece, piece, precision=lax.Precision.HIGHEST)
        imag_vis = jnp.einsum('pcaf,qcaf->pq', swapped, piece, precision=lax.Precision.HIGHEST)
        vis_group = jnp.stack([real_vis, imag_vis]) * scale
        gains = lax.dynamic_slice_in_dim(calib, start, AVG, 1).astype(jnp.float32)
        gain_real = jnp.transpose(gains[0])[:, :, None]
        gain_imag = jnp.transpose(gains[1])[:, :, None]
        volt_real = piece[:, 0]
        volt_imag = piece[:, 1]
        cal_real = (gain_real * volt_real - gain_imag * volt_imag).astype(jnp.bfloat16)
        cal_imag = (gain_real * volt_imag + gain_imag * volt_real).astype(jnp.bfloat16)
        cal_real, cal_imag = lax.optimization_barrier((cal_real, cal_imag))
        cal_real = cal_real.astype(jnp.float32)
        cal_imag = cal_imag.astype(jnp.float32)
        first_pair = jnp.stack([cal_real, -cal_imag], axis=1)
        second_pair = jnp.stack([cal_imag, cal_real], axis=1)
        real_beam = jnp.einsum('bcp,pcaf->abf', weights, first_pair, precision=lax.Precision.HIGHEST)
        imag_beam = jnp.einsum('bcp,pcaf->abf', weights, second_pair, precision=lax.Precision.HIGHEST)
        beam_group = jnp.stack([real_beam, imag_beam]).astype(jnp.bfloat16)
        return vis_group, beam_group

    vis_all, beam_all = lax.map(per_group, jnp.arange(VIS, dtype=jnp.int32))
    visibility = jnp.transpose(vis_all, (1, 0, 2, 3))
    beams = jnp.transpose(beam_all, (1, 0, 2, 3, 4)).reshape(2, KEPT, BEAMS, FRAMES)
    return visibility, beams
```

```python
import functools
import math

import jax
import jax.numpy as jnp
import numpy as np
from jax import lax
from jax.experimental import pallas as pl
from jax.experimental.pallas import tpu as pltpu
from jax.sharding import PartitionSpec as P

LANES = 128
HALF = 16
BLOCKS = 32
ROWS = 80
MESH = pl.DeviceIdType.MESH


def twiddles():
    k = np.arange(BLOCKS)[:, None].astype(np.float64)
    lane = np.arange(LANES)[None, :].astype(np.float64)
    angle = 2.0 * np.pi / 4096.0 * k * lane
    return np.stack([np.cos(angle), -np.sin(angle)]).astype(np.float32)


def lane_matrix(band_start):
    bins = (band_start[:, None] // 32 + jnp.arange(2, dtype=jnp.int32)[None, :]).reshape(-1)
    turn = (bins[:, None] * jnp.arange(LANES, dtype=jnp.int32)[None, :]) % LANES
    angle = (2.0 * math.pi / LANES) * turn.astype(jnp.float32)
    cosine = jnp.cos(angle) / 64.0
    sine = jnp.sin(angle) / 64.0
    upper = jnp.concatenate([cosine, sine], axis=1)
    lower = jnp.concatenate([-sine, cosine], axis=1)
    return jnp.concatenate([upper, lower], axis=0).astype(jnp.bfloat16)


def cmul_const(re, im, angle):
    c, s = math.cos(angle), math.sin(angle)
    if abs(s) < 1e-12 and c > 0:
        return re, im
    if abs(c) < 1e-12:
        return (im, -re) if s > 0 else (-im, re)
    if abs(abs(c) - abs(s)) < 1e-12 and c > 0 and s > 0:
        return (re + im) * c, (im - re) * c
    if abs(abs(c) - abs(s)) < 1e-12 and c < 0 and s > 0:
        return (im - re) * s, (im + re) * (-s)
    return re * c + im * s, im * c - re * s


def dft4(x):
    (ar, ai), (br, bi), (cr, ci), (dr, di) = x
    pr, pi = ar + cr, ai + ci
    qr, qi = ar - cr, ai - ci
    rr, ri = br + dr, bi + di
    sr, si = br - dr, bi - di
    return [
        (pr + rr, pi + ri),
        (qr + si, qi - sr),
        (pr - rr, pi - ri),
        (qr - si, qi + sr),
    ]


def dft8(x):
    even = dft4(x[0::2])
    odd = dft4(x[1::2])
    odd = [cmul_const(r, i, 2.0 * math.pi * k / 8.0) for k, (r, i) in enumerate(odd)]
    low = [(e[0] + o[0], e[1] + o[1]) for e, o in zip(even, odd)]
    high = [(e[0] - o[0], e[1] - o[1]) for e, o in zip(even, odd)]
    return low + high


def spectra_kernel(
    volt, taps, tw, mat, out, vbuf, stage, ybuf, tbuf, sbuf, load_sems, send_sems, recv_sems
):
    me_c = lax.axis_index("chan")
    me_s = lax.axis_index("sect")
    n_c = lax.axis_size("chan")
    n_s = lax.axis_size("sect")
    count = n_c * n_s
    frames = volt.shape[2] // 4096

    def load(half, f):
        return pltpu.make_async_copy(
            volt.at[:, pl.ds(half * HALF, HALF), pl.ds(f * 4096, 4096)],
            vbuf.at[half, f + 3],
            load_sems.at[half],
        )

    for half in range(2):

        @pl.loop(0, frames)
        def _(f):
            load(half, f).start()

    barrier = pltpu.get_barrier_semaphore()

    def peer(step):
        return (
            lax.rem(me_c + step // n_s, n_c),
            lax.rem(me_s + lax.rem(step, n_s), n_s),
        )

    @pl.loop(1, count)
    def _(step):
        pl.semaphore_signal(barrier, inc=1, device_id=peer(step), device_id_type=MESH)

    for half in range(2):
        for pad in range(3):
            vbuf[half, pad] = jnp.zeros(vbuf.shape[2:], vbuf.dtype)
            vbuf[half, frames + 3 + pad] = jnp.zeros(vbuf.shape[2:], vbuf.dtype)

    @pl.loop(0, 2)
    def _(half):
        pltpu.make_async_copy(
            vbuf.at[half, pl.ds(3, frames)], vbuf.at[half, pl.ds(3, frames)], load_sems.at[half]
        ).wait()

        @pl.loop(0, frames + 3)
        def _(f):
            for q0 in range(8):
                four = []
                for q1 in range(4):
                    cols = pl.ds((q0 + 8 * q1) * LANES, LANES)
                    parts = []
                    for part in range(2):
                        total = None
                        for t in range(4):
                            x = vbuf[half, f + 3 - t, part, :, cols].astype(jnp.float32)
                            term = x * taps[t : t + 1, cols]
                            total = term if total is None else total + term
                        parts.append(total)
                    four.append(tuple(parts))
                for ka, (re, im) in enumerate(dft4(four)):
                    re, im = cmul_const(re, im, 2.0 * math.pi * q0 * ka / 32.0)
                    stage[ka, q0, 0] = re
                    stage[ka, q0, 1] = im
            for ka in range(4):
                eight = [(stage[ka, q0, 0], stage[ka, q0, 1]) for q0 in range(8)]
                for kb, (re, im) in enumerate(dft8(eight)):
                    k = ka + 4 * kb
                    c = tw[0, k : k + 1, :]
                    s = tw[1, k : k + 1, :]
                    rows = pl.ds(k * HALF, HALF)
                    ybuf[rows, :LANES] = (re * c - im * s).astype(jnp.bfloat16)
                    ybuf[rows, LANES:] = (re * s + im * c).astype(jnp.bfloat16)
            own = f < frames
            for group in range(4):
                k_hi, kh = group // 2, group % 2
                res = lax.dot_general(
                    mat[...],
                    ybuf[group * LANES : (group + 1) * LANES, :],
                    (((1,), (1,)), ((), ())),
                    preferred_element_type=jnp.float32,
                )
                for part in range(2):
                    base = jnp.where(
                        own,
                        k_hi * ROWS + kh * 32 + part * 16 + f,
                        k_hi * ROWS + 64 + kh * 8 + part * 4 + f - frames,
                    )
                    tbuf[pl.ds(base, 64, stride=2 * ROWS), :] = res[part * 64 : (part + 1) * 64]

        @pl.when(half == 0)
        def _():
            pl.semaphore_wait(barrier, count - 1)

        slot = me_s * n_c + me_c

        @pl.loop(0, count)
        def _(step):
            c, s = peer(step)
            dest = c * n_s + s
            block = tbuf[pl.ds(pl.multiple_of(dest * ROWS, 8), ROWS), :]
            sbuf[half, dest] = block.astype(jnp.bfloat16)

            @pl.when(step > 0)
            def _():
                pltpu.make_async_remote_copy(
                    src_ref=sbuf.at[half, dest],
                    dst_ref=out.at[half, slot],
                    send_sem=send_sems.at[half],
                    recv_sem=recv_sems.at[half],
                    device_id=(c, s),
                    device_id_type=MESH,
                ).start()

            @pl.when(step == 0)
            def _():
                pltpu.make_async_copy(
                    sbuf.at[half, dest], out.at[half, slot], recv_sems.at[half]
                ).start()

    for half in range(2):
        pltpu.make_async_copy(out.at[half], out.at[half], recv_sems.at[half]).wait()
        pltpu.make_async_copy(
            sbuf.at[half, pl.ds(0, count - 1)],
            sbuf.at[half, pl.ds(0, count - 1)],
            send_sems.at[half],
        ).wait()


def channelize(voltages, fir_taps, band_start):
    count = lax.axis_size("chan") * lax.axis_size("sect")
    frames = voltages.shape[2] // 4096
    hbm = pl.BlockSpec(memory_space=pl.ANY)
    vmem = pl.BlockSpec(memory_space=pltpu.VMEM)
    return pl.pallas_call(
        spectra_kernel,
        out_shape=jax.ShapeDtypeStruct((2, count, ROWS, LANES), jnp.bfloat16),
        in_specs=[hbm, vmem, vmem, vmem],
        out_specs=hbm,
        scratch_shapes=[
            pltpu.VMEM((2, frames + 6, 2, HALF, 4096), jnp.bfloat16),
            pltpu.VMEM((4, 8, 2, HALF, LANES), jnp.float32),
            pltpu.VMEM((BLOCKS * HALF, 2 * LANES), jnp.bfloat16),
            pltpu.VMEM((count * ROWS, LANES), jnp.float32),
            pltpu.VMEM((2, count, ROWS, LANES), jnp.bfloat16),
            pltpu.SemaphoreType.DMA((2,)),
            pltpu.SemaphoreType.DMA((2,)),
            pltpu.SemaphoreType.DMA((2,)),
        ],
        compiler_params=pltpu.CompilerParams(
            collective_id=0, has_side_effects=True, vmem_limit_bytes=56 * 1024 * 1024
        ),
        name="spectra",
    )(voltages, fir_taps, jnp.asarray(twiddles()), lane_matrix(band_start))


def swap_blocks(tiles):
    lane = lax.broadcasted_iota(jnp.int32, tiles[0].shape, 1)
    tiles = list(tiles)
    for bit in (4, 2, 1):
        upper = (lane // (bit * 16)) % 2 == 1
        for j in range(8):
            if j & bit == 0:
                a, b = tiles[j], tiles[j + bit]
                tiles[j] = jnp.where(upper, pltpu.roll(b, bit * 16, 1), a)
                tiles[j + bit] = jnp.where(upper, b, pltpu.roll(a, LANES - bit * 16, 1))
    return tiles


NT = (((1,), (1,)), ((), ()))


def dot_nt(a, b):
    return lax.dot_general(a, b, NT, preferred_element_type=jnp.float32)


def product_kernel(
    scale, recv, order, calib, steer, pick, vis, beams, xt, ct, gains, weights, zbuf, wbuf
):
    n_s = 8
    n_c = 16

    @pl.when(pl.program_id(0) == 0)
    def _():
        gains[...] = jnp.dot(calib[...], order[...], preferred_element_type=jnp.float32)
        picked = jnp.dot(pick[...], steer[...], preferred_element_type=jnp.float32)
        picked = picked.astype(jnp.bfloat16)
        for part in range(2):
            weights[part * 512 : (part + 1) * 512, :] = jnp.dot(
                picked[:, part * 512 : (part + 1) * 512],
                order[...],
                preferred_element_type=jnp.float32,
            ).astype(jnp.bfloat16)

        @pl.loop(0, n_s)
        def _(s):
            before = jnp.maximum(s - 1, 0)
            row = lax.broadcasted_iota(jnp.int32, (8, LANES), 0)
            keep = (row < 3) & (s > 0)
            for half in range(2):
                for c_hi in range(2):
                    group = half * 2 + c_hi
                    cols = slice(group * LANES, (group + 1) * LANES)
                    for kh in range(2):
                        done = []
                        for part in range(2):
                            tiles = []
                            for c_lo in range(8):
                                c = c_hi * 8 + c_lo
                                rows = pl.ds((kh * 2 + part) * 16, 16)
                                own = recv[half, s * n_c + c, rows, :].astype(jnp.float32)
                                extra = recv[half, before * n_c + c, 64:80, :]
                                extra = extra.astype(jnp.float32)[kh * 8 : kh * 8 + 8]
                                if part == 1:
                                    extra = pltpu.roll(extra, 4, 0)
                                first = own[:8] + jnp.where(keep, extra, 0.0)
                                tiles.append(jnp.concatenate([first, own[8:]], axis=0))
                            done.append(swap_blocks(tiles))
                        for k8 in range(8):
                            ch = kh * 8 + k8
                            real = done[0][k8].astype(jnp.bfloat16)
                            imag = done[1][k8].astype(jnp.bfloat16)
                            low = pl.ds(pl.multiple_of(s * 16, 16), 16)
                            high = pl.ds(pl.multiple_of(128 + s * 16, 16), 16)
                            xt[ch, low, cols] = real
                            xt[ch, high, cols] = imag
                            real = real.astype(jnp.float32)
                            imag = imag.astype(jnp.float32)
                            g_re = gains[ch : ch + 1, cols]
                            g_im = gains[16 + ch : 17 + ch, cols]
                            ct[ch, low, cols] = (g_re * real - g_im * imag).astype(jnp.bfloat16)
                            ct[ch, high, cols] = (g_re * imag + g_im * real).astype(jnp.bfloat16)

    g = pl.program_id(0)
    for a in range(4):
        z = dot_nt(order[...], xt[g * 4 + a]).astype(jnp.bfloat16)
        zbuf[:, a * 256 : (a + 1) * 256] = z
        wbuf[:, a * 256 : a * 256 + 128] = z[:, 128:]
        wbuf[:, a * 256 + 128 : (a + 1) * 256] = -z[:, :128]
    vis[0, 0] = dot_nt(zbuf[...], zbuf[...]) * scale
    vis[1, 0] = dot_nt(wbuf[...], zbuf[...]) * scale
    n_b = beams.shape[2]
    for a in range(4):
        uv = dot_nt(weights[...], ct[g * 4 + a])
        beams[0, a] = (uv[:n_b, :128] - uv[512 : 512 + n_b, 128:]).astype(jnp.bfloat16)
        beams[1, a] = (uv[:n_b, 128:] + uv[512 : 512 + n_b, :128]).astype(jnp.bfloat16)


def products(received, station_map, calib, table, beam_index):
    rank = jnp.arange(512, dtype=jnp.int32)
    row_of = (rank // 16 % 16) * 32 + (rank // 256) * 16 + rank % 16
    place = station_map.reshape(16, 2, 16).transpose(1, 0, 2).reshape(-1)
    del row_of
    order = (place[None, :] == rank[:, None]).astype(jnp.bfloat16)
    padded = jnp.pad(beam_index, (0, 12), constant_values=-1)
    pick = (padded[:, None] == jnp.arange(1024, dtype=jnp.int32)[None, :]).astype(jnp.bfloat16)
    whole = lambda *dims: pl.BlockSpec(dims, lambda g: (0,) * len(dims))
    return pl.pallas_call(
        functools.partial(product_kernel, 1.0 / 512.0),
        grid=(4,),
        out_shape=(
            jax.ShapeDtypeStruct((2, 4, 512, 512), jnp.float32),
            jax.ShapeDtypeStruct((2, 16, 500, 128), jnp.bfloat16),
        ),
        in_specs=[
            whole(2, 128, ROWS, LANES),
            whole(512, 512),
            whole(32, 512),
            whole(1024, 1024),
            whole(512, 1024),
        ],
        out_specs=(
            pl.BlockSpec((2, 1, 512, 512), lambda g: (0, g, 0, 0)),
            pl.BlockSpec((2, 4, 500, 128), lambda g: (0, g, 0, 0)),
        ),
        scratch_shapes=[
            pltpu.VMEM((16, 256, 512), jnp.bfloat16),
            pltpu.VMEM((16, 256, 512), jnp.bfloat16),
            pltpu.VMEM((32, 512), jnp.float32),
            pltpu.VMEM((1024, 512), jnp.bfloat16),
            pltpu.VMEM((512, 1024), jnp.bfloat16),
            pltpu.VMEM((512, 1024), jnp.bfloat16),
        ],
        compiler_params=pltpu.CompilerParams(vmem_limit_bytes=56 * 1024 * 1024),
        name="products",
    )(received, order, calib.reshape(32, 512), table.reshape(1024, 1024), pick)


def shards(voltages, fir_taps, station_map, band_start, calib, steer, beam_index):
    table = lax.all_gather(steer, "sect", axis=0, tiled=True)
    received = channelize(voltages, fir_taps, band_start)
    return products(received, station_map, calib, table, beam_index)


def solution(mesh):
    return jax.shard_map(
        shards,
        mesh=mesh,
        in_specs=(
            P(None, "chan", "sect"),
            P(),
            P(),
            P(),
            P(None, ("chan", "sect"), None),
            P("sect", None, None),
            P(),
        ),
        out_specs=(P(None, ("chan", "sect"), None, None), P(None, ("chan", "sect"), None, None)),
        check_vma=False,
    )
```

```python
import functools
import math

import jax
import jax.numpy as jnp
import numpy as np
from jax import lax
from jax.experimental import pallas as pl
from jax.experimental.pallas import tpu as pltpu
from jax.sharding import PartitionSpec as P

LANES = 128
HALF = 16
BLOCKS = 32
ROWS = 80
MESH = pl.DeviceIdType.MESH


def twiddles():
    k = np.arange(BLOCKS)[:, None].astype(np.float64)
    lane = np.arange(LANES)[None, :].astype(np.float64)
    angle = 2.0 * np.pi / 4096.0 * k * lane
    return np.stack([np.cos(angle), -np.sin(angle)]).astype(np.float32)


def lane_matrix(band_start):
    bins = (band_start[:, None] // 32 + jnp.arange(2, dtype=jnp.int32)[None, :]).reshape(-1)
    turn = (bins[:, None] * jnp.arange(LANES, dtype=jnp.int32)[None, :]) % LANES
    angle = (2.0 * math.pi / LANES) * turn.astype(jnp.float32)
    cosine = jnp.cos(angle) / 64.0
    sine = jnp.sin(angle) / 64.0
    upper = jnp.concatenate([cosine, sine], axis=1)
    lower = jnp.concatenate([-sine, cosine], axis=1)
    return jnp.concatenate([upper, lower], axis=0).astype(jnp.bfloat16)


def cmul_const(re, im, angle):
    c, s = math.cos(angle), math.sin(angle)
    if abs(s) < 1e-12 and c > 0:
        return re, im
    if abs(c) < 1e-12:
        return (im, -re) if s > 0 else (-im, re)
    if abs(abs(c) - abs(s)) < 1e-12 and c > 0 and s > 0:
        return (re + im) * c, (im - re) * c
    if abs(abs(c) - abs(s)) < 1e-12 and c < 0 and s > 0:
        return (im - re) * s, (im + re) * (-s)
    return re * c + im * s, im * c - re * s


def dft4(x):
    (ar, ai), (br, bi), (cr, ci), (dr, di) = x
    pr, pi = ar + cr, ai + ci
    qr, qi = ar - cr, ai - ci
    rr, ri = br + dr, bi + di
    sr, si = br - dr, bi - di
    return [
        (pr + rr, pi + ri),
        (qr + si, qi - sr),
        (pr - rr, pi - ri),
        (qr - si, qi + sr),
    ]


def dft8(x):
    even = dft4(x[0::2])
    odd = dft4(x[1::2])
    odd = [cmul_const(r, i, 2.0 * math.pi * k / 8.0) for k, (r, i) in enumerate(odd)]
    low = [(e[0] + o[0], e[1] + o[1]) for e, o in zip(even, odd)]
    high = [(e[0] - o[0], e[1] - o[1]) for e, o in zip(even, odd)]
    return low + high


NT = (((1,), (1,)), ((), ()))
TN = (((0,), (0,)), ((), ()))


def dot(a, b, dims=(((1,), (0,)), ((), ()))):
    return lax.dot_general(a, b, dims, preferred_element_type=jnp.float32)


def iota(shape, dim):
    return lax.broadcasted_iota(jnp.int32, shape, dim)


def one_hot(found):
    return jnp.where(found, 1.0, 0.0).astype(jnp.bfloat16)


def spectra_kernel(
    volt, steer, emat, taps, tw, mat, smap, bidx, calib,
    xt_out, ct_out, w_out, order_out,
    vbuf, stage, ybuf, tbuf, sbuf, rbuf, xin, res, ebuf, xt, ct, order, gains, table, wpart,
    wall, weights, load_sems, send_sems, recv_sems, steer_sems, out_sems,
):
    me_c = lax.axis_index("chan")
    me_s = lax.axis_index("sect")
    n_c = lax.axis_size("chan")
    n_s = lax.axis_size("sect")
    count = n_c * n_s
    frames = volt.shape[2] // 4096
    core = lax.rem(me_c, 2)
    chip = me_c // 2
    my_x = lax.rem(chip, 2) * 2 + me_s // 4
    my_y = lax.rem(me_s, 4)
    my_z = chip // 2

    def load(half, f):
        return pltpu.make_async_copy(
            volt.at[:, pl.ds(half * HALF, HALF), pl.ds(f * 4096, 4096)],
            vbuf.at[half, f + 3],
            load_sems.at[half],
        )

    for half in range(2):

        @pl.loop(0, frames)
        def _(f):
            load(half, f).start()

    fetch_e = pltpu.make_async_copy(emat, ebuf, steer_sems.at[4])
    fetch_e.start()

    barrier = pltpu.get_barrier_semaphore()

    @pl.loop(1, count)
    def _(step):
        c = lax.rem(me_c + step // n_s, n_c)
        s = lax.rem(me_s + lax.rem(step, n_s), n_s)
        pl.semaphore_signal(barrier, inc=1, device_id=(c, s), device_id_type=MESH)

    for half in range(2):
        for pad in range(3):
            vbuf[half, pad] = jnp.zeros(vbuf.shape[2:], vbuf.dtype)
            vbuf[half, frames + 3 + pad] = jnp.zeros(vbuf.shape[2:], vbuf.dtype)

    pl.semaphore_wait(barrier, count - 1)

    share = steer.at[:, pl.ds(pl.multiple_of(chip * LANES, LANES), LANES)]

    @pl.loop(1, n_s)
    def _(step):
        pltpu.make_async_remote_copy(
            src_ref=share,
            dst_ref=table.at[me_s],
            send_sem=steer_sems.at[0],
            recv_sem=steer_sems.at[1],
            device_id=(me_c, lax.rem(me_s + step, n_s)),
            device_id_type=MESH,
        ).start()

    pltpu.make_async_copy(share, table.at[me_s], steer_sems.at[1]).start()

    def pick_and_share():
        pltpu.make_async_copy(table, table, steer_sems.at[1]).wait()
        total = None
        for s in range(8):
            found = bidx[...] == iota((LANES, 512), 0) + s * LANES
            term = dot(one_hot(found), table[s], TN)
            total = term if total is None else total + term
        wpart[...] = total.astype(jnp.bfloat16)

        @pl.loop(1, 8)
        def _(step):
            pltpu.make_async_remote_copy(
                src_ref=wpart,
                dst_ref=wall.at[chip],
                send_sem=steer_sems.at[2],
                recv_sem=steer_sems.at[3],
                device_id=(lax.rem(chip + step, 8) * 2 + core, me_s),
                device_id_type=MESH,
            ).start()

        pltpu.make_async_copy(wpart, wall.at[chip], steer_sems.at[3]).start()

    def one_frame(half, f):
        for q0 in range(8):
            four = []
            for q1 in range(4):
                cols = pl.ds((q0 + 8 * q1) * LANES, LANES)
                parts = []
                for part in range(2):
                    total = None
                    for t in range(4):
                        x = vbuf[half, f + 3 - t, part, :, cols].astype(jnp.float32)
                        term = x * taps[t : t + 1, cols]
                        total = term if total is None else total + term
                    parts.append(total)
                four.append(tuple(parts))
            for ka, (re, im) in enumerate(dft4(four)):
                re, im = cmul_const(re, im, 2.0 * math.pi * q0 * ka / 32.0)
                stage[ka, q0, 0] = re
                stage[ka, q0, 1] = im
        for ka in range(4):
            eight = [(stage[ka, q0, 0], stage[ka, q0, 1]) for q0 in range(8)]
            for kb, (re, im) in enumerate(dft8(eight)):
                k = ka + 4 * kb
                c = tw[0, k : k + 1, :]
                s = tw[1, k : k + 1, :]
                rows = pl.ds(k * HALF, HALF)
                ybuf[rows, :LANES] = (re * c - im * s).astype(jnp.bfloat16)
                ybuf[rows, LANES:] = (re * s + im * c).astype(jnp.bfloat16)
        own = f < frames
        for group in range(4):
            k_hi, kh = group // 2, group % 2
            out = dot(mat[...], ybuf[group * LANES : (group + 1) * LANES, :], NT)
            for part in range(2):
                base = k_hi * ROWS + jnp.where(
                    own,
                    f // 8 * 32 + kh * 16 + part * 8 + lax.rem(f, 8),
                    64 + kh * 8 + part * 4 + f - frames,
                )
                tbuf[pl.ds(base, 64, stride=2 * ROWS), :] = out[part * 64 : (part + 1) * 64]

    slot = me_s * n_c + me_c

    def send_out(half, late):
        rows = pl.ds(32, 48) if late else pl.ds(0, 32)

        @pl.loop(0, count // 2)
        def _(step):
            k0 = lax.rem(step, 4)
            k1 = lax.rem(step // 4, 4)
            k2 = step // 16
            x = lax.rem(my_x + k0, 4)
            y = lax.rem(my_y + k0 + k1, 4)
            z = lax.rem(my_z + k0 + k1 + k2, 4)
            for flip in range(2):
                c = (z * 2 + x // 2) * 2 + lax.rem(core + flip, 2)
                s = lax.rem(x, 2) * 4 + y
                dest = c * n_s + s
                first = pl.multiple_of(dest * ROWS + (32 if late else 0), 8)
                block = tbuf[pl.ds(first, 48 if late else 32), :]
                sbuf[half, dest, rows] = block.astype(jnp.bfloat16)

                def go():
                    pltpu.make_async_remote_copy(
                        src_ref=sbuf.at[half, dest, rows],
                        dst_ref=rbuf.at[half, slot, rows],
                        send_sem=send_sems.at[half, late],
                        recv_sem=recv_sems.at[half, late],
                        device_id=(c, s),
                        device_id_type=MESH,
                    ).start()

                if flip:
                    go()
                else:
                    pl.when(step > 0)(go)

                    @pl.when(step == 0)
                    def _():
                        pltpu.make_async_copy(
                            sbuf.at[half, dest, rows],
                            rbuf.at[half, slot, rows],
                            recv_sems.at[half, late],
                        ).start()

    @pl.loop(0, 2)
    def _(half):
        pltpu.make_async_copy(
            vbuf.at[half, pl.ds(3, frames)], vbuf.at[half, pl.ds(3, frames)], load_sems.at[half]
        ).wait()

        @pl.loop(0, 8)
        def _(f):
            one_frame(half, f)

            @pl.when((half == 0) & (f == 4))
            def _():
                pick_and_share()

        send_out(half, 0)

        @pl.loop(8, frames + 3)
        def _(f):
            one_frame(half, f)

        send_out(half, 1)

    rank = iota((512, 512), 1)
    natural = lax.rem(rank // 16, 16) * 32 + rank // 256 * 16 + lax.rem(rank, 16)
    move = one_hot(iota((512, 512), 0) == natural)
    order[...] = dot(one_hot(smap[...] == iota((512, 512), 0)), move).astype(jnp.bfloat16)
    gains[...] = dot(calib[...], order[...])
    pltpu.make_async_copy(wall, wall, steer_sems.at[3]).wait()
    for part in range(2):
        picked = jnp.concatenate([wall[part * 4 + j] for j in range(4)], axis=1)
        weights[part * 512 : (part + 1) * 512, :] = dot(picked, order[...]).astype(jnp.bfloat16)
    put = [
        pltpu.make_async_copy(weights, w_out, out_sems.at[0]),
        pltpu.make_async_copy(order, order_out, out_sems.at[1]),
    ]
    for copy in put:
        copy.start()
    fetch_e.wait()

    row = iota((8, LANES), 0)
    for half in range(2):
        for late in range(2):
            rows = pl.ds(32, 48) if late else pl.ds(0, 32)
            pltpu.make_async_copy(
                rbuf.at[half, :, rows], rbuf.at[half, :, rows], recv_sems.at[half, late]
            ).wait()
        for c_hi in range(2):
            cols = slice(half * 256 + c_hi * LANES, half * 256 + (c_hi + 1) * LANES)
            for kh in range(2):

                @pl.loop(0, n_s)
                def _(s):
                    before = jnp.maximum(s - 1, 0)
                    keep = (row < 3) & (s > 0)
                    low = pl.ds(pl.multiple_of(s * 32, 32), 16)
                    high = pl.ds(pl.multiple_of(s * 32 + 16, 16), 16)
                    for c_lo in range(8):
                        c = c_hi * 8 + c_lo
                        at = s * n_c + c
                        lanes = slice(c_lo * LANES, (c_lo + 1) * LANES)
                        early = rbuf[half, at, kh * 16 : kh * 16 + 16].astype(jnp.float32)
                        extra = rbuf[half, before * n_c + c, 64:80].astype(jnp.float32)
                        extra = extra[kh * 8 : kh * 8 + 8]
                        extra = jnp.concatenate(
                            [
                                jnp.where(keep, extra, 0.0),
                                jnp.where(keep, pltpu.roll(extra, 4, 0), 0.0),
                            ],
                            axis=0,
                        )
                        xin[low, lanes] = (early + extra).astype(jnp.bfloat16)
                        xin[high, lanes] = rbuf[half, at, 32 + kh * 16 : 48 + kh * 16]

                res[...] = dot(xin[...], ebuf[...])

                @pl.loop(0, n_s)
                def _(s):
                    low = pl.ds(pl.multiple_of(s * 16, 16), 16)
                    high = pl.ds(pl.multiple_of(128 + s * 16, 16), 16)
                    for k8 in range(8):
                        ch = kh * 8 + k8
                        lanes = slice(k8 * LANES, (k8 + 1) * LANES)
                        quarter = [
                            res[pl.ds(pl.multiple_of(s * 32 + 8 * j, 8), 8), lanes]
                            for j in range(4)
                        ]
                        real = jnp.concatenate([quarter[0], quarter[2]], axis=0)
                        imag = jnp.concatenate([quarter[1], quarter[3]], axis=0)
                        xt[ch, low, cols] = real.astype(jnp.bfloat16)
                        xt[ch, high, cols] = imag.astype(jnp.bfloat16)
                        g_re = gains[ch : ch + 1, cols]
                        g_im = gains[16 + ch : 17 + ch, cols]
                        ct[ch, low, cols] = (g_re * real - g_im * imag).astype(jnp.bfloat16)
                        ct[ch, high, cols] = (g_re * imag + g_im * real).astype(jnp.bfloat16)

        cols = pl.ds(half * 256, 256)
        for k, (src, dst) in enumerate(((xt, xt_out), (ct, ct_out))):
            put.append(
                pltpu.make_async_copy(
                    src.at[:, :, cols], dst.at[:, :, cols], out_sems.at[2 + half * 2 + k]
                )
            )
            put[-1].start()

    for copy in put:
        copy.wait()
    for half in range(2):
        for late in range(2):
            rows = pl.ds(32, 48) if late else pl.ds(0, 32)
            sent = sbuf.at[half, pl.ds(0, count - 1), rows]
            pltpu.make_async_copy(sent, sent, send_sems.at[half, late]).wait()
    sent = table.at[pl.ds(0, 7)]
    pltpu.make_async_copy(sent, sent, steer_sems.at[0]).wait()
    sent = wall.at[pl.ds(0, 7)]
    pltpu.make_async_copy(sent, sent, steer_sems.at[2]).wait()


def block_swap():
    line = np.arange(1024)
    source = (line // 16 % 8) * LANES + (line // LANES) * 16 + line % 16
    out = np.zeros((1024, 1024), np.float32)
    out[source, line] = 1.0
    return out.astype(jnp.bfloat16)


def channelize(voltages, fir_taps, band_start, steer, station_map, beam_index, calib):
    count = lax.axis_size("chan") * lax.axis_size("sect")
    frames = voltages.shape[2] // 4096
    hbm = pl.BlockSpec(memory_space=pl.ANY)
    vmem = pl.BlockSpec(memory_space=pltpu.VMEM)
    half16 = jnp.bfloat16
    return pl.pallas_call(
        spectra_kernel,
        out_shape=(
            jax.ShapeDtypeStruct((16, 256, 512), half16),
            jax.ShapeDtypeStruct((16, 256, 512), half16),
            jax.ShapeDtypeStruct((1024, 512), half16),
            jax.ShapeDtypeStruct((512, 512), half16),
        ),
        in_specs=[hbm] * 3 + [vmem] * 6,
        out_specs=(hbm,) * 4,
        scratch_shapes=[
            pltpu.VMEM((2, frames + 6, 2, HALF, 4096), half16),
            pltpu.VMEM((4, 8, 2, HALF, LANES), jnp.float32),
            pltpu.VMEM((BLOCKS * HALF, 2 * LANES), half16),
            pltpu.VMEM((count * ROWS, LANES), jnp.float32),
            pltpu.VMEM((2, count, ROWS, LANES), half16),
            pltpu.VMEM((2, count, ROWS, LANES), half16),
            pltpu.VMEM((256, 1024), half16),
            pltpu.VMEM((256, 1024), jnp.float32),
            pltpu.VMEM((1024, 1024), half16),
            pltpu.VMEM((16, 256, 512), half16),
            pltpu.VMEM((16, 256, 512), half16),
            pltpu.VMEM((512, 512), half16),
            pltpu.VMEM((32, 512), jnp.float32),
            pltpu.VMEM((8, LANES, LANES), half16),
            pltpu.VMEM((512, LANES), half16),
            pltpu.VMEM((8, 512, LANES), half16),
            pltpu.VMEM((1024, 512), half16),
            pltpu.SemaphoreType.DMA((2,)),
            pltpu.SemaphoreType.DMA((2, 2)),
            pltpu.SemaphoreType.DMA((2, 2)),
            pltpu.SemaphoreType.DMA((5,)),
            pltpu.SemaphoreType.DMA((6,)),
        ],
        compiler_params=pltpu.CompilerParams(
            collective_id=0, has_side_effects=True, vmem_limit_bytes=60 * 1024 * 1024
        ),
        name="spectra",
    )(
        voltages,
        steer.reshape(LANES, 1024),
        jnp.asarray(block_swap()),
        fir_taps,
        jnp.asarray(twiddles()),
        lane_matrix(band_start),
        station_map.reshape(1, 512),
        jnp.pad(beam_index, (0, 12), constant_values=-1).reshape(1, 512),
        calib.reshape(32, 512),
    )


def product_kernel(scale, xt, ct, weights, order, vis, beams, zbuf, wbuf, bbuf, obuf, sem):
    step = pl.program_id(0)
    n_b = beams.shape[1]
    tiles = bbuf.shape[0]

    def put(part):
        return pltpu.make_async_copy(
            obuf.at[part, pl.ds(0, n_b)], beams.at[part], sem.at[part]
        )

    @pl.when(step < 4)
    def _():
        for a in range(4):
            uv = dot(weights[...], ct[a], NT)
            real = uv[:512, :128] - uv[512:, 128:]
            imag = uv[:512, 128:] + uv[512:, :128]
            both = jnp.concatenate([real, imag], axis=1).astype(jnp.bfloat16)
            rows = pl.ds(pl.multiple_of(step * 64 + a * 16, 16), 16)
            bbuf[:, rows, :] = both.reshape(tiles, 16, 256)

    @pl.when(step == 3)
    def _():
        line = iota((256, 256), 0)
        source = lax.rem(line, 16) * 16 + line // 16
        move = one_hot(iota((256, 256), 1) == source)

        @pl.loop(0, tiles)
        def _(tile):
            out = dot(move, bbuf[tile]).astype(jnp.bfloat16)
            for part in range(2):
                piece = out[:, part * 128 : (part + 1) * 128].reshape(16, 16, 128)
                obuf[part, pl.ds(tile * 16, 16)] = piece

        for part in range(2):
            put(part).start()

    @pl.when(step >= 4)
    def _():
        for a in range(4):
            z = dot(order[...], xt[a], NT).astype(jnp.bfloat16)
            zbuf[:, a * 256 : (a + 1) * 256] = z
            wbuf[:, a * 256 : a * 256 + 128] = z[:, 128:]
            wbuf[:, a * 256 + 128 : (a + 1) * 256] = -z[:, :128]
        vis[0, 0] = dot(zbuf[...], zbuf[...], NT) * scale
        vis[1, 0] = dot(wbuf[...], zbuf[...], NT) * scale

    @pl.when(step == 7)
    def _():
        for part in range(2):
            put(part).wait()


def products(xt, ct, weights, order):
    half16 = jnp.bfloat16
    vis, beams = pl.pallas_call(
        functools.partial(product_kernel, 1.0 / 512.0),
        grid=(8,),
        out_shape=(
            jax.ShapeDtypeStruct((2, 4, 512, 512), jnp.float32),
            jax.ShapeDtypeStruct((2, 500, 16, 128), half16),
        ),
        in_specs=[
            pl.BlockSpec((4, 256, 512), lambda i: (jnp.maximum(i - 4, 0), 0, 0)),
            pl.BlockSpec((4, 256, 512), lambda i: (jnp.minimum(i, 3), 0, 0)),
            pl.BlockSpec((1024, 512), lambda i: (0, 0)),
            pl.BlockSpec((512, 512), lambda i: (0, 0)),
        ],
        out_specs=(
            pl.BlockSpec((2, 1, 512, 512), lambda i: (0, jnp.maximum(i - 4, 0), 0, 0)),
            pl.BlockSpec(memory_space=pl.ANY),
        ),
        scratch_shapes=[
            pltpu.VMEM((512, 1024), half16),
            pltpu.VMEM((512, 1024), half16),
            pltpu.VMEM((32, 256, 256), half16),
            pltpu.VMEM((2, 512, 16, 128), half16),
            pltpu.SemaphoreType.DMA((2,)),
        ],
        compiler_params=pltpu.CompilerParams(vmem_limit_bytes=56 * 1024 * 1024),
        name="products",
    )(xt, ct, weights, order)
    return vis, jnp.transpose(beams, (0, 2, 1, 3))


def shards(voltages, fir_taps, station_map, band_start, calib, steer, beam_index):
    parts = channelize(
        voltages, fir_taps, band_start, steer, station_map, beam_index, calib
    )
    return products(*parts)


def solution(mesh):
    return jax.shard_map(
        shards,
        mesh=mesh,
        in_specs=(
            P(None, "chan", "sect"),
            P(),
            P(),
            P(),
            P(None, ("chan", "sect"), None),
            P("sect", None, None),
            P(),
        ),
        out_specs=(P(None, ("chan", "sect"), None, None), P(None, ("chan", "sect"), None, None)),
        check_vma=False,
    )
```

```python
import functools
import math

import jax
import jax.numpy as jnp
import numpy as np
from jax import lax
from jax.experimental import pallas as pl
from jax.experimental.pallas import tpu as pltpu
from jax.sharding import PartitionSpec as P

LANES = 128
HALF = 16
BLOCKS = 32
ROWS = 80
PITCH = 81
MESH = pl.DeviceIdType.MESH


def twiddles():
    k = np.arange(BLOCKS)[:, None].astype(np.float64)
    lane = np.arange(LANES)[None, :].astype(np.float64)
    angle = 2.0 * np.pi / 4096.0 * k * lane
    return np.stack([np.cos(angle), -np.sin(angle)]).astype(np.float32)


def lane_table():
    bins = np.arange(LANES)
    angle = 2.0 * np.pi / LANES * (bins[:, None] * bins[None, :] % LANES)
    cosine, sine = np.cos(angle) / 64.0, np.sin(angle) / 64.0
    return np.block([[cosine, sine], [-sine, cosine]]).astype(np.float32)


def cmul_const(re, im, angle):
    c, s = math.cos(angle), math.sin(angle)
    if abs(s) < 1e-12 and c > 0:
        return re, im
    if abs(c) < 1e-12:
        return (im, -re) if s > 0 else (-im, re)
    if abs(abs(c) - abs(s)) < 1e-12 and c > 0 and s > 0:
        return (re + im) * c, (im - re) * c
    if abs(abs(c) - abs(s)) < 1e-12 and c < 0 and s > 0:
        return (im - re) * s, (im + re) * (-s)
    return re * c + im * s, im * c - re * s


def dft4(x):
    (ar, ai), (br, bi), (cr, ci), (dr, di) = x
    pr, pi = ar + cr, ai + ci
    qr, qi = ar - cr, ai - ci
    rr, ri = br + dr, bi + di
    sr, si = br - dr, bi - di
    return [
        (pr + rr, pi + ri),
        (qr + si, qi - sr),
        (pr - rr, pi - ri),
        (qr - si, qi + sr),
    ]


def dft8(x):
    even = dft4(x[0::2])
    odd = dft4(x[1::2])
    odd = [cmul_const(r, i, 2.0 * math.pi * k / 8.0) for k, (r, i) in enumerate(odd)]
    low = [(e[0] + o[0], e[1] + o[1]) for e, o in zip(even, odd)]
    high = [(e[0] - o[0], e[1] - o[1]) for e, o in zip(even, odd)]
    return low + high


NT = (((1,), (1,)), ((), ()))
TN = (((0,), (0,)), ((), ()))


def dot(a, b, dims=(((1,), (0,)), ((), ()))):
    return lax.dot_general(a, b, dims, preferred_element_type=jnp.float32)


def iota(shape, dim):
    return lax.broadcasted_iota(jnp.int32, shape, dim)


def one_hot(found):
    return jnp.where(found, 1.0, 0.0).astype(jnp.bfloat16)


def spectra_kernel(
    volt, steer, taps, tw, lines, bands, smap, beam, calib,
    xt, ct, weights, order,
    vbuf, stage, ybuf, tbuf, sbuf, rbuf, xin, res, ebuf, gains, table, wpart, wall, mat, bidx,
    load_sems, send_sems, recv_sems, steer_sems,
):
    me_c = lax.axis_index("chan")
    me_s = lax.axis_index("sect")
    n_c = lax.axis_size("chan")
    n_s = lax.axis_size("sect")
    count = n_c * n_s
    frames = volt.shape[2] // 4096
    core = lax.rem(me_c, 2)
    chip = me_c // 2
    my_x = lax.rem(chip, 2) * 2 + me_s // 4
    my_y = lax.rem(me_s, 4)
    my_z = chip // 2

    def load(half, f):
        return pltpu.make_async_copy(
            volt.at[:, pl.ds(half * HALF, HALF), pl.ds(f * 4096, 4096)],
            vbuf.at[half, f + 3],
            load_sems.at[half, f // 8],
        )

    for half in range(2):

        @pl.loop(0, frames)
        def _(f):
            load(half, f).start()

    barrier = pltpu.get_barrier_semaphore()

    @pl.loop(1, count)
    def _(step):
        c = lax.rem(me_c + step // n_s, n_c)
        s = lax.rem(me_s + lax.rem(step, n_s), n_s)
        pl.semaphore_signal(barrier, inc=1, device_id=(c, s), device_id_type=MESH)

    for half in range(2):
        for pad in range(3):
            vbuf[half, pad] = jnp.zeros(vbuf.shape[2:], vbuf.dtype)
            vbuf[half, frames + 3 + pad] = jnp.zeros(vbuf.shape[2:], vbuf.dtype)

    column = iota((32, LANES), 1)
    spread = one_hot(lax.rem(column, 64) // 2 == iota((32, LANES), 0))
    number = jnp.broadcast_to(bands[...] // 64, (8, 32)).astype(jnp.float32)
    column = iota((8, LANES), 1)
    wanted = dot(number.astype(jnp.bfloat16), spread).astype(jnp.int32) * 2
    wanted = wanted + lax.rem(column, 2) + column // 64 * LANES
    mat[...] = dot(
        one_hot(wanted[:1] == iota((2 * LANES, LANES), 0)), lines[...].astype(jnp.bfloat16), TN
    ).astype(jnp.bfloat16)
    bidx[...] = jnp.full(bidx.shape, -1, jnp.int32)
    bidx[:, : beam.shape[1]] = beam[...]

    pl.semaphore_wait(barrier, count - 1)

    mine = my_z * 2 + core
    share = steer.at[:, pl.ds(pl.multiple_of(mine * LANES, LANES), LANES)]

    @pl.loop(1, n_s)
    def _(step):
        pltpu.make_async_remote_copy(
            src_ref=share,
            dst_ref=table.at[me_s],
            send_sem=steer_sems.at[0],
            recv_sem=steer_sems.at[1],
            device_id=(me_c, lax.rem(me_s + step, n_s)),
            device_id_type=MESH,
        ).start()

    pltpu.make_async_copy(share, table.at[me_s], steer_sems.at[1]).start()

    def pick_and_share():
        pltpu.make_async_copy(table, table, steer_sems.at[1]).wait()
        total = None
        for s in range(8):
            found = bidx[...] == iota((LANES, 512), 0) + s * LANES
            term = dot(one_hot(found), table[s], TN)
            total = term if total is None else total + term
        wpart[...] = total.astype(jnp.bfloat16)

        @pl.loop(1, 4)
        def _(step):
            pltpu.make_async_remote_copy(
                src_ref=wpart,
                dst_ref=wall.at[mine],
                send_sem=steer_sems.at[2],
                recv_sem=steer_sems.at[3],
                device_id=(lax.rem(me_c + step * 4, n_c), me_s),
                device_id_type=MESH,
            ).start()

        pltpu.make_async_remote_copy(
            src_ref=wpart,
            dst_ref=wall.at[mine],
            send_sem=steer_sems.at[2],
            recv_sem=steer_sems.at[4],
            device_id=(me_c + 1 - 2 * core, me_s),
            device_id_type=MESH,
        ).start()
        pltpu.make_async_copy(wpart, wall.at[mine], steer_sems.at[3]).start()

    def pass_on():
        four = wall.at[pl.ds(0, 4)]
        pltpu.make_async_copy(four, four, steer_sems.at[3]).wait()

        @pl.loop(1, 4)
        def _(step):
            other = lax.rem(my_z + step, 4) * 2 + core
            pltpu.make_async_remote_copy(
                src_ref=wall.at[other],
                dst_ref=wall.at[other],
                send_sem=steer_sems.at[5],
                recv_sem=steer_sems.at[4],
                device_id=(me_c + 1 - 2 * core, me_s),
                device_id_type=MESH,
            ).start()

    def one_frame(half, f):
        for q0 in range(8):
            four = []
            for q1 in range(4):
                cols = pl.ds((q0 + 8 * q1) * LANES, LANES)
                parts = []
                for part in range(2):
                    total = None
                    for t in range(4):
                        x = vbuf[half, f + 3 - t, part, :, cols].astype(jnp.float32)
                        term = x * taps[t : t + 1, cols]
                        total = term if total is None else total + term
                    parts.append(total)
                four.append(tuple(parts))
            for ka, (re, im) in enumerate(dft4(four)):
                re, im = cmul_const(re, im, 2.0 * math.pi * q0 * ka / 32.0)
                stage[ka, q0, 0] = re
                stage[ka, q0, 1] = im
        for ka in range(4):
            eight = [(stage[ka, q0, 0], stage[ka, q0, 1]) for q0 in range(8)]
            for kb, (re, im) in enumerate(dft8(eight)):
                k = ka + 4 * kb
                c = tw[0, k : k + 1, :]
                s = tw[1, k : k + 1, :]
                rows = pl.ds(k * HALF, HALF)
                ybuf[rows, :LANES] = (re * c - im * s).astype(jnp.bfloat16)
                ybuf[rows, LANES:] = (re * s + im * c).astype(jnp.bfloat16)
        own = f < frames
        for group in range(4):
            k_hi, kh = group // 2, group % 2
            out = dot(mat[...], ybuf[group * LANES : (group + 1) * LANES, :], NT)
            for part in range(2):
                base = k_hi * 64 * PITCH + jnp.where(
                    own,
                    f // 8 * 48 + kh * 16 + part * 8 + lax.rem(f, 8),
                    32 + kh * 8 + part * 4 + f - frames,
                )
                tbuf[pl.ds(base, 64, stride=PITCH), :] = out[part * 64 : (part + 1) * 64]

    slot = me_s * n_c + me_c

    def message_rows(half, late):
        cut = 48 if half else 32
        return pl.ds(cut, ROWS - cut) if late else pl.ds(0, cut)

    def send_out(half, late):
        rows = message_rows(half, late)

        @pl.loop(0, count // 2)
        def _(step):
            k0 = lax.rem(step, 4)
            k1 = lax.rem(step // 4, 4)
            k2 = step // 16
            x = lax.rem(my_x + k0, 4)
            y = lax.rem(my_y + k0 + k1, 4)
            z = lax.rem(my_z + k0 + k1 + k2, 4)
            for flip in range(2):
                c = (z * 2 + x // 2) * 2 + lax.rem(core + flip, 2)
                s = lax.rem(x, 2) * 4 + y
                dest = c * n_s + s
                first = (lax.rem(dest, 2) * 64 + dest // 2) * PITCH + rows.start
                block = tbuf[pl.ds(first, rows.size), :]
                sbuf[half, dest, rows] = block.astype(jnp.bfloat16)

                def go():
                    pltpu.make_async_remote_copy(
                        src_ref=sbuf.at[half, dest, rows],
                        dst_ref=rbuf.at[half, slot, rows],
                        send_sem=send_sems.at[half, late],
                        recv_sem=recv_sems.at[half, late],
                        device_id=(c, s),
                        device_id_type=MESH,
                    ).start()

                if flip:
                    go()
                else:
                    pl.when(step > 0)(go)

                    @pl.when(step == 0)
                    def _():
                        pltpu.make_async_copy(
                            sbuf.at[half, dest, rows],
                            rbuf.at[half, slot, rows],
                            recv_sems.at[half, late],
                        ).start()

    def arrived(half, late):
        part = vbuf.at[half, pl.ds(3 + 8 * late, 8)]
        pltpu.make_async_copy(part, part, load_sems.at[half, late]).wait()

    arrived(0, 0)

    @pl.loop(0, 8)
    def _(f):
        one_frame(0, f)

    send_out(0, 0)
    pick_and_share()
    arrived(0, 1)

    @pl.loop(8, frames + 3)
    def _(f):
        one_frame(0, f)

    send_out(0, 1)
    pass_on()
    arrived(1, 0)
    arrived(1, 1)

    @pl.loop(0, 11)
    def _(i):
        one_frame(1, jnp.where(i < 8, i, i + 8))

    send_out(1, 0)

    @pl.loop(8, frames)
    def _(f):
        one_frame(1, f)

    send_out(1, 1)

    rank = iota((512, 512), 1)
    natural = lax.rem(rank // 16, 16) * 32 + rank // 256 * 16 + lax.rem(rank, 16)
    move = one_hot(iota((512, 512), 0) == natural)
    order[...] = dot(one_hot(smap[...] == iota((512, 512), 0)), move).astype(jnp.bfloat16)
    gains[...] = dot(calib[...], order[...])
    line = iota((1024, 1024), 1)
    source = lax.rem(line // 16, 8) * LANES + line // LANES * 16 + lax.rem(line, 16)
    ebuf[...] = one_hot(iota((1024, 1024), 0) == source)
    four = wall.at[pl.ds(0, 4)]
    pltpu.make_async_copy(four, four, steer_sems.at[4]).wait()
    for part in range(2):
        picked = jnp.concatenate([wall[part * 4 + j] for j in range(4)], axis=1)
        weights[part * 512 : (part + 1) * 512, :] = dot(picked, order[...]).astype(jnp.bfloat16)

    row = iota((8, LANES), 0)
    for half in range(2):
        for late in range(2):
            rows = message_rows(half, late)
            pltpu.make_async_copy(
                rbuf.at[half, :, rows], rbuf.at[half, :, rows], recv_sems.at[half, late]
            ).wait()
            if late < 1 - half:
                continue
            for fh in (late,) if half else (0, 1):
                for kh in range(2):
                    for c_hi in range(2):
                        at_row = (kh * 2 + c_hi) * LANES

                        @pl.loop(0, n_s)
                        def _(s):
                            before = jnp.maximum(s - 1, 0)
                            keep = (row < 3) & (s > 0)
                            there = pl.ds(pl.multiple_of(at_row + s * 16, 16), 16)
                            for c_lo in range(8):
                                c = c_hi * 8 + c_lo
                                lanes = slice(c_lo * LANES, (c_lo + 1) * LANES)
                                at = fh * 48 + kh * 16
                                piece = rbuf[half, s * n_c + c, at : at + 16]
                                if fh == 0:
                                    extra = rbuf[half, before * n_c + c, 32:48]
                                    extra = extra.astype(jnp.float32)[kh * 8 : kh * 8 + 8]
                                    extra = jnp.concatenate(
                                        [
                                            jnp.where(keep, extra, 0.0),
                                            jnp.where(keep, pltpu.roll(extra, 4, 0), 0.0),
                                        ],
                                        axis=0,
                                    )
                                    piece = piece.astype(jnp.float32) + extra
                                xin[there, lanes] = piece.astype(jnp.bfloat16)

                res[fh] = dot(xin[...], ebuf[...])

        for kh in range(2):
            for c_hi in range(2):
                cols = slice(half * 256 + c_hi * LANES, half * 256 + (c_hi + 1) * LANES)
                at_row = (kh * 2 + c_hi) * LANES

                @pl.loop(0, n_s)
                def _(s):
                    low = pl.ds(pl.multiple_of(s * 16, 16), 16)
                    high = pl.ds(pl.multiple_of(128 + s * 16, 16), 16)
                    first = pl.ds(pl.multiple_of(at_row + s * 16, 8), 8)
                    second = pl.ds(pl.multiple_of(at_row + s * 16 + 8, 8), 8)
                    for k8 in range(8):
                        ch = kh * 8 + k8
                        lanes = slice(k8 * LANES, (k8 + 1) * LANES)
                        real = jnp.concatenate([res[0, first, lanes], res[1, first, lanes]], axis=0)
                        imag = jnp.concatenate(
                            [res[0, second, lanes], res[1, second, lanes]], axis=0
                        )
                        xt[ch, low, cols] = real.astype(jnp.bfloat16)
                        xt[ch, high, cols] = imag.astype(jnp.bfloat16)
                        g_re = gains[ch : ch + 1, cols]
                        g_im = gains[16 + ch : 17 + ch, cols]
                        ct[ch, low, cols] = (g_re * real - g_im * imag).astype(jnp.bfloat16)
                        ct[ch, high, cols] = (g_re * imag + g_im * real).astype(jnp.bfloat16)

    for half in range(2):
        for late in range(2):
            sent = sbuf.at[half, pl.ds(0, count - 1), message_rows(half, late)]
            pltpu.make_async_copy(sent, sent, send_sems.at[half, late]).wait()
    sent = table.at[pl.ds(0, 7)]
    pltpu.make_async_copy(sent, sent, steer_sems.at[0]).wait()
    sent = wall.at[pl.ds(0, 4)]
    pltpu.make_async_copy(sent, sent, steer_sems.at[2]).wait()
    sent = wall.at[pl.ds(0, 3)]
    pltpu.make_async_copy(sent, sent, steer_sems.at[5]).wait()


def channelize(voltages, fir_taps, band_start, steer, station_map, beam_index, calib):
    count = lax.axis_size("chan") * lax.axis_size("sect")
    frames = voltages.shape[2] // 4096
    hbm = pl.BlockSpec(memory_space=pl.ANY)
    vmem = pl.BlockSpec(memory_space=pltpu.VMEM)
    half16 = jnp.bfloat16
    return pl.pallas_call(
        spectra_kernel,
        out_shape=(
            pltpu.VMEM((16, 256, 512), half16),
            pltpu.VMEM((16, 256, 512), half16),
            pltpu.VMEM((1024, 512), half16),
            pltpu.VMEM((512, 512), half16),
        ),
        in_specs=[hbm] * 2 + [vmem] * 7,
        out_specs=(vmem,) * 4,
        scratch_shapes=[
            pltpu.VMEM((2, frames + 6, 2, HALF, 4096), half16),
            pltpu.VMEM((4, 8, 2, HALF, LANES), jnp.float32),
            pltpu.VMEM((BLOCKS * HALF, 2 * LANES), half16),
            pltpu.VMEM((count * PITCH, LANES), jnp.float32),
            pltpu.VMEM((2, count, ROWS, LANES), half16),
            pltpu.VMEM((2, count, ROWS, LANES), half16),
            pltpu.VMEM((512, 1024), half16),
            pltpu.VMEM((2, 512, 1024), jnp.float32),
            pltpu.VMEM((1024, 1024), half16),
            pltpu.VMEM((32, 512), jnp.float32),
            pltpu.VMEM((8, LANES, LANES), half16),
            pltpu.VMEM((512, LANES), half16),
            pltpu.VMEM((8, 512, LANES), half16),
            pltpu.VMEM((LANES, 2 * LANES), half16),
            pltpu.VMEM((1, 512), jnp.int32),
            pltpu.SemaphoreType.DMA((2, 2)),
            pltpu.SemaphoreType.DMA((2, 2)),
            pltpu.SemaphoreType.DMA((2, 2)),
            pltpu.SemaphoreType.DMA((6,)),
        ],
        compiler_params=pltpu.CompilerParams(
            collective_id=0, has_side_effects=True, vmem_limit_bytes=48 * 1024 * 1024
        ),
        name="spectra",
    )(
        voltages,
        steer.reshape(LANES, 1024),
        fir_taps,
        jnp.asarray(twiddles()),
        jnp.asarray(lane_table()),
        band_start.reshape(1, 32),
        station_map.reshape(1, 512),
        beam_index.reshape(1, -1),
        calib.reshape(32, 512),
    )


def product_kernel(
    scale, xt, ct, weights, order, vis, beams, zbuf, wbuf, bbuf, obuf, pbuf, beam_sems, vis_sems
):
    n_b = beams.shape[1]
    tiles = bbuf.shape[0]

    @pl.loop(0, xt.shape[0])
    def _(ch):
        uv = dot(weights[...], ct[ch], NT)
        real = uv[:512, :128] - uv[512:, 128:]
        imag = uv[:512, 128:] + uv[512:, :128]
        both = jnp.concatenate([real, imag], axis=1).astype(jnp.bfloat16)
        rows = pl.ds(pl.multiple_of(ch * 16, 16), 16)
        bbuf[:, rows, :] = both.reshape(tiles, 16, 256)

    line = iota((256, 256), 0)
    source = lax.rem(line, 16) * 16 + line // 16
    move = one_hot(iota((256, 256), 1) == source)

    @pl.loop(0, tiles // 4)
    def _(four):
        for j in range(4):
            tile = four * 4 + j
            out = dot(move, bbuf[tile]).astype(jnp.bfloat16)
            for part in range(2):
                piece = out[:, part * 128 : (part + 1) * 128].reshape(16, 16, 128)
                obuf[part, pl.ds(tile * 16, 16)] = piece

    def put_beams(part):
        return pltpu.make_async_copy(
            obuf.at[part, pl.ds(0, n_b)], beams.at[part], beam_sems.at[part]
        )

    def put_vis(part, g):
        return pltpu.make_async_copy(pbuf.at[part, g % 2], vis.at[part, g], vis_sems.at[part, g % 2])

    for part in range(2):
        put_beams(part).start()

    for g in range(4):
        for a in range(4):
            z = dot(order[...], xt[g * 4 + a], NT).astype(jnp.bfloat16)
            zbuf[:, a * 256 : (a + 1) * 256] = z
            wbuf[:, a * 256 : a * 256 + 128] = z[:, 128:]
            wbuf[:, a * 256 + 128 : (a + 1) * 256] = -z[:, :128]
        for part, left in enumerate((zbuf, wbuf)):
            if g >= 2:
                put_vis(part, g - 2).wait()
            pbuf[part, g % 2] = dot(left[...], zbuf[...], NT) * scale
            put_vis(part, g).start()

    for part in range(2):
        for g in (2, 3):
            put_vis(part, g).wait()
        put_beams(part).wait()


def products(xt, ct, weights, order):
    half16 = jnp.bfloat16
    hbm = pl.BlockSpec(memory_space=pl.ANY)
    vmem = pl.BlockSpec(memory_space=pltpu.VMEM)
    vis, beams = pl.pallas_call(
        functools.partial(product_kernel, 1.0 / 512.0),
        out_shape=(
            jax.ShapeDtypeStruct((2, 4, 512, 512), jnp.float32),
            jax.ShapeDtypeStruct((2, 500, 16, 128), half16),
        ),
        in_specs=[vmem] * 4,
        out_specs=(hbm, hbm),
        scratch_shapes=[
            pltpu.VMEM((512, 1024), half16),
            pltpu.VMEM((512, 1024), half16),
            pltpu.VMEM((32, 256, 256), half16),
            pltpu.VMEM((2, 512, 16, 128), half16),
            pltpu.VMEM((2, 2, 512, 512), jnp.float32),
            pltpu.SemaphoreType.DMA((2,)),
            pltpu.SemaphoreType.DMA((2, 2)),
        ],
        compiler_params=pltpu.CompilerParams(vmem_limit_bytes=40 * 1024 * 1024),
        name="products",
    )(xt, ct, weights, order)
    return vis, jnp.transpose(beams, (0, 2, 1, 3))


def shards(voltages, fir_taps, station_map, band_start, calib, steer, beam_index):
    parts = channelize(
        voltages, fir_taps, band_start, steer, station_map, beam_index, calib
    )
    return products(*parts)


def solution(mesh):
    return jax.shard_map(
        shards,
        mesh=mesh,
        in_specs=(
            P(None, "chan", "sect"),
            P(),
            P(),
            P(),
            P(None, ("chan", "sect"), None),
            P("sect", None, None),
            P(),
        ),
        out_specs=(P(None, ("chan", "sect"), None, None), P(None, ("chan", "sect"), None, None)),
        check_vma=False,
    )
```

```python
import functools
import math

import jax
import jax.numpy as jnp
import numpy as np
from jax import lax
from jax.experimental import pallas as pl
from jax.experimental.pallas import tpu as pltpu
from jax.sharding import PartitionSpec as P

LANES = 128
HALF = 16
BLOCKS = 32
ROWS = 80
PITCH = 81
MESH = pl.DeviceIdType.MESH


def twiddles():
    k = np.arange(BLOCKS)[:, None].astype(np.float64)
    lane = np.arange(LANES)[None, :].astype(np.float64)
    angle = 2.0 * np.pi / 4096.0 * k * lane
    return np.stack([np.cos(angle), -np.sin(angle)]).astype(np.float32)


def lane_table():
    bins = np.arange(LANES)
    angle = 2.0 * np.pi / LANES * (bins[:, None] * bins[None, :] % LANES)
    cosine, sine = np.cos(angle) / 64.0, np.sin(angle) / 64.0
    return np.block([[cosine, sine], [-sine, cosine]]).astype(np.float32)


def cmul_const(re, im, angle):
    c, s = math.cos(angle), math.sin(angle)
    if abs(s) < 1e-12 and c > 0:
        return re, im
    if abs(c) < 1e-12:
        return (im, -re) if s > 0 else (-im, re)
    if abs(abs(c) - abs(s)) < 1e-12 and c > 0 and s > 0:
        return (re + im) * c, (im - re) * c
    if abs(abs(c) - abs(s)) < 1e-12 and c < 0 and s > 0:
        return (im - re) * s, (im + re) * (-s)
    return re * c + im * s, im * c - re * s


def dft4(x):
    (ar, ai), (br, bi), (cr, ci), (dr, di) = x
    pr, pi = ar + cr, ai + ci
    qr, qi = ar - cr, ai - ci
    rr, ri = br + dr, bi + di
    sr, si = br - dr, bi - di
    return [
        (pr + rr, pi + ri),
        (qr + si, qi - sr),
        (pr - rr, pi - ri),
        (qr - si, qi + sr),
    ]


def dft8(x):
    even = dft4(x[0::2])
    odd = dft4(x[1::2])
    odd = [cmul_const(r, i, 2.0 * math.pi * k / 8.0) for k, (r, i) in enumerate(odd)]
    low = [(e[0] + o[0], e[1] + o[1]) for e, o in zip(even, odd)]
    high = [(e[0] - o[0], e[1] - o[1]) for e, o in zip(even, odd)]
    return low + high


NT = (((1,), (1,)), ((), ()))
TN = (((0,), (0,)), ((), ()))


def dot(a, b, dims=(((1,), (0,)), ((), ()))):
    return lax.dot_general(a, b, dims, preferred_element_type=jnp.float32)


def iota(shape, dim):
    return lax.broadcasted_iota(jnp.int32, shape, dim)


def one_hot(found):
    return jnp.where(found, 1.0, 0.0).astype(jnp.bfloat16)


def spectra_kernel(
    volt, steer, taps, tw, lines, bands, smap, beam, calib,
    xt, ct, weights, order,
    vbuf, stage, ybuf, tbuf, sbuf, rbuf, xin, res, ebuf, gains, table, wpart, wall, mat, bidx,
    pick,
    load_sems, send_sems, recv_sems, steer_sems,
):
    me_c = lax.axis_index("chan")
    me_s = lax.axis_index("sect")
    n_c = lax.axis_size("chan")
    n_s = lax.axis_size("sect")
    count = n_c * n_s
    frames = volt.shape[2] // 4096
    core = lax.rem(me_c, 2)
    chip = me_c // 2
    my_x = lax.rem(chip, 2) * 2 + me_s // 4
    my_y = lax.rem(me_s, 4)
    my_z = chip // 2

    def load(half, f):
        return pltpu.make_async_copy(
            volt.at[:, pl.ds(half * HALF, HALF), pl.ds(f * 4096, 4096)],
            vbuf.at[half, f + 3],
            load_sems.at[half, f // 8],
        )

    for half in range(2):

        @pl.loop(0, frames)
        def _(f):
            load(half, f).start()

    barrier = pltpu.get_barrier_semaphore()

    @pl.loop(1, count)
    def _(step):
        c = lax.rem(me_c + step // n_s, n_c)
        s = lax.rem(me_s + lax.rem(step, n_s), n_s)
        pl.semaphore_signal(barrier, inc=1, device_id=(c, s), device_id_type=MESH)

    for half in range(2):
        for pad in range(3):
            vbuf[half, pad] = jnp.zeros(vbuf.shape[2:], vbuf.dtype)
            vbuf[half, frames + 3 + pad] = jnp.zeros(vbuf.shape[2:], vbuf.dtype)

    column = iota((32, LANES), 1)
    spread = one_hot(lax.rem(column, 64) // 2 == iota((32, LANES), 0))
    number = jnp.broadcast_to(bands[...] // 64, (8, 32)).astype(jnp.float32)
    column = iota((8, LANES), 1)
    wanted = dot(number.astype(jnp.bfloat16), spread).astype(jnp.int32) * 2
    wanted = wanted + lax.rem(column, 2) + column // 64 * LANES
    mat[...] = dot(
        one_hot(wanted[:1] == iota((2 * LANES, LANES), 0)), lines[...].astype(jnp.bfloat16), TN
    ).astype(jnp.bfloat16)
    bidx[...] = jnp.full(bidx.shape, -1, jnp.int32)
    bidx[:, : beam.shape[1]] = beam[...]

    pl.semaphore_wait(barrier, count - 1)
    mine = my_z * 2 + core
    share = steer.at[:, pl.ds(pl.multiple_of(mine * LANES, LANES), LANES)]

    @pl.loop(1, n_s)
    def _(step):
        pltpu.make_async_remote_copy(
            src_ref=share,
            dst_ref=table.at[me_s],
            send_sem=steer_sems.at[0],
            recv_sem=steer_sems.at[1],
            device_id=(me_c, lax.rem(me_s + step, n_s)),
            device_id_type=MESH,
        ).start()

    pltpu.make_async_copy(share, table.at[me_s], steer_sems.at[1]).start()

    entry = jnp.broadcast_to(bidx[...].astype(jnp.float32), (LANES, 512)).T
    entry = entry.astype(jnp.int32)
    for s in range(8):
        pick[:, s * LANES : (s + 1) * LANES] = one_hot(entry == iota((512, LANES), 1) + s * LANES)

    def pick_and_share():
        pltpu.make_async_copy(table, table, steer_sems.at[1]).wait()
        wpart[...] = dot(pick[...], table[...].reshape(8 * LANES, LANES)).astype(jnp.bfloat16)

        @pl.loop(1, 4)
        def _(step):
            pltpu.make_async_remote_copy(
                src_ref=wpart,
                dst_ref=wall.at[mine],
                send_sem=steer_sems.at[2],
                recv_sem=steer_sems.at[3],
                device_id=(lax.rem(me_c + step * 4, n_c), me_s),
                device_id_type=MESH,
            ).start()

        pltpu.make_async_remote_copy(
            src_ref=wpart,
            dst_ref=wall.at[mine],
            send_sem=steer_sems.at[2],
            recv_sem=steer_sems.at[4],
            device_id=(me_c + 1 - 2 * core, me_s),
            device_id_type=MESH,
        ).start()
        pltpu.make_async_copy(wpart, wall.at[mine], steer_sems.at[3]).start()

    def pass_on():
        four = wall.at[pl.ds(0, 4)]
        pltpu.make_async_copy(four, four, steer_sems.at[3]).wait()

        @pl.loop(1, 4)
        def _(step):
            other = lax.rem(my_z + step, 4) * 2 + core
            pltpu.make_async_remote_copy(
                src_ref=wall.at[other],
                dst_ref=wall.at[other],
                send_sem=steer_sems.at[5],
                recv_sem=steer_sems.at[4],
                device_id=(me_c + 1 - 2 * core, me_s),
                device_id_type=MESH,
            ).start()

    def one_frame(half, f):
        for q0 in range(8):
            four = []
            for q1 in range(4):
                cols = pl.ds((q0 + 8 * q1) * LANES, LANES)
                parts = []
                for part in range(2):
                    total = None
                    for t in range(4):
                        x = vbuf[half, f + 3 - t, part, :, cols].astype(jnp.float32)
                        term = x * taps[t : t + 1, cols]
                        total = term if total is None else total + term
                    parts.append(total)
                four.append(tuple(parts))
            for ka, (re, im) in enumerate(dft4(four)):
                re, im = cmul_const(re, im, 2.0 * math.pi * q0 * ka / 32.0)
                stage[ka, q0, 0] = re
                stage[ka, q0, 1] = im
        for ka in range(4):
            eight = [(stage[ka, q0, 0], stage[ka, q0, 1]) for q0 in range(8)]
            for kb, (re, im) in enumerate(dft8(eight)):
                k = ka + 4 * kb
                c = tw[0, k : k + 1, :]
                s = tw[1, k : k + 1, :]
                rows = pl.ds(k * HALF, HALF)
                ybuf[rows, :LANES] = (re * c - im * s).astype(jnp.bfloat16)
                ybuf[rows, LANES:] = (re * s + im * c).astype(jnp.bfloat16)
        own = f < frames
        for group in range(4):
            k_hi, kh = group // 2, group % 2
            out = dot(mat[...], ybuf[group * LANES : (group + 1) * LANES, :], NT)
            for part in range(2):
                base = k_hi * 64 * PITCH + jnp.where(
                    own,
                    f // 8 * 48 + kh * 16 + part * 8 + lax.rem(f, 8),
                    32 + kh * 8 + part * 4 + f - frames,
                )
                tbuf[pl.ds(base, 64, stride=PITCH), :] = out[part * 64 : (part + 1) * 64]

    slot = me_s * n_c + me_c

    def message_rows(half, late):
        cut = 48 if half else 32
        return pl.ds(cut, ROWS - cut) if late else pl.ds(0, cut)

    def send_out(half, late):
        rows = message_rows(half, late)

        @pl.loop(0, count // 2, unroll=2)
        def _(step):
            k0 = lax.rem(step, 4)
            k1 = lax.rem(step // 4, 4)
            k2 = step // 16
            x = lax.rem(my_x + k0, 4)
            y = lax.rem(my_y + k0 + k1, 4)
            z = lax.rem(my_z + k0 + k1 + k2, 4)
            for flip in range(2):
                c = (z * 2 + x // 2) * 2 + lax.rem(core + flip, 2)
                s = lax.rem(x, 2) * 4 + y
                dest = c * n_s + s
                first = (lax.rem(dest, 2) * 64 + dest // 2) * PITCH + rows.start
                block = tbuf[pl.ds(first, rows.size), :]
                sbuf[half, dest, rows] = block.astype(jnp.bfloat16)

                def go():
                    pltpu.make_async_remote_copy(
                        src_ref=sbuf.at[half, dest, rows],
                        dst_ref=rbuf.at[half, slot, rows],
                        send_sem=send_sems.at[half, late],
                        recv_sem=recv_sems.at[half, late],
                        device_id=(c, s),
                        device_id_type=MESH,
                    ).start()

                if flip:
                    go()
                else:
                    pl.when(step > 0)(go)

                    @pl.when(step == 0)
                    def _():
                        pltpu.make_async_copy(
                            sbuf.at[half, dest, rows],
                            rbuf.at[half, slot, rows],
                            recv_sems.at[half, late],
                        ).start()

    def arrived(half, late):
        part = vbuf.at[half, pl.ds(3 + 8 * late, 8)]
        pltpu.make_async_copy(part, part, load_sems.at[half, late]).wait()

    arrived(0, 0)

    @pl.loop(0, 3)
    def _(f):
        one_frame(0, f)

    pick_and_share()

    @pl.loop(3, 8)
    def _(f):
        one_frame(0, f)

    send_out(0, 0)
    arrived(0, 1)

    @pl.loop(8, frames + 3)
    def _(f):
        one_frame(0, f)

    send_out(0, 1)
    pass_on()
    arrived(1, 0)
    arrived(1, 1)

    @pl.loop(0, 11)
    def _(i):
        one_frame(1, jnp.where(i < 8, i, i + 8))

    send_out(1, 0)

    @pl.loop(8, frames)
    def _(f):
        one_frame(1, f)

    send_out(1, 1)

    rank = iota((512, 512), 1)
    natural = lax.rem(rank // 16, 16) * 32 + rank // 256 * 16 + lax.rem(rank, 16)
    move = one_hot(iota((512, 512), 0) == natural)
    order[...] = dot(one_hot(smap[...] == iota((512, 512), 0)), move).astype(jnp.bfloat16)
    gains[...] = dot(calib[...], order[...])
    line = iota((1024, 1024), 1)
    source = lax.rem(line // 16, 8) * LANES + line // LANES * 16 + lax.rem(line, 16)
    ebuf[...] = one_hot(iota((1024, 1024), 0) == source)
    four = wall.at[pl.ds(0, 4)]
    pltpu.make_async_copy(four, four, steer_sems.at[4]).wait()
    for part in range(2):
        picked = jnp.concatenate([wall[part * 4 + j] for j in range(4)], axis=1)
        weights[part * 512 : (part + 1) * 512, :] = dot(picked, order[...]).astype(jnp.bfloat16)

    row = iota((8, LANES), 0)
    for half in range(2):
        for late in range(2):
            rows = message_rows(half, late)
            pltpu.make_async_copy(
                rbuf.at[half, :, rows], rbuf.at[half, :, rows], recv_sems.at[half, late]
            ).wait()
            if late < 1 - half:
                continue
            for fh in (late,) if half else (0, 1):
                for kh in range(2):
                    for c_hi in range(2):
                        at_row = (kh * 2 + c_hi) * LANES

                        @pl.loop(0, n_s)
                        def _(s):
                            before = jnp.maximum(s - 1, 0)
                            keep = (row < 3) & (s > 0)
                            there = pl.ds(pl.multiple_of(at_row + s * 16, 16), 16)
                            for c_lo in range(8):
                                c = c_hi * 8 + c_lo
                                lanes = slice(c_lo * LANES, (c_lo + 1) * LANES)
                                at = fh * 48 + kh * 16
                                piece = rbuf[half, s * n_c + c, at : at + 16]
                                if fh == 0:
                                    extra = rbuf[half, before * n_c + c, 32:48]
                                    extra = extra.astype(jnp.float32)[kh * 8 : kh * 8 + 8]
                                    extra = jnp.concatenate(
                                        [
                                            jnp.where(keep, extra, 0.0),
                                            jnp.where(keep, pltpu.roll(extra, 4, 0), 0.0),
                                        ],
                                        axis=0,
                                    )
                                    piece = piece.astype(jnp.float32) + extra
                                xin[there, lanes] = piece.astype(jnp.bfloat16)

                res[fh] = dot(xin[...], ebuf[...])

        for kh in range(2):
            for c_hi in range(2):
                cols = slice(half * 256 + c_hi * LANES, half * 256 + (c_hi + 1) * LANES)
                at_row = (kh * 2 + c_hi) * LANES

                @pl.loop(0, n_s)
                def _(s):
                    low = pl.ds(pl.multiple_of(s * 16, 16), 16)
                    high = pl.ds(pl.multiple_of(128 + s * 16, 16), 16)
                    first = pl.ds(pl.multiple_of(at_row + s * 16, 8), 8)
                    second = pl.ds(pl.multiple_of(at_row + s * 16 + 8, 8), 8)
                    for k8 in range(8):
                        ch = kh * 8 + k8
                        lanes = slice(k8 * LANES, (k8 + 1) * LANES)
                        real = jnp.concatenate([res[0, first, lanes], res[1, first, lanes]], axis=0)
                        imag = jnp.concatenate(
                            [res[0, second, lanes], res[1, second, lanes]], axis=0
                        )
                        xt[ch, low, cols] = real.astype(jnp.bfloat16)
                        xt[ch, high, cols] = imag.astype(jnp.bfloat16)
                        g_re = gains[ch : ch + 1, cols]
                        g_im = gains[16 + ch : 17 + ch, cols]
                        ct[ch, low, cols] = (g_re * real - g_im * imag).astype(jnp.bfloat16)
                        ct[ch, high, cols] = (g_re * imag + g_im * real).astype(jnp.bfloat16)

    for half in range(2):
        for late in range(2):
            sent = sbuf.at[half, pl.ds(0, count - 1), message_rows(half, late)]
            pltpu.make_async_copy(sent, sent, send_sems.at[half, late]).wait()
    sent = table.at[pl.ds(0, 7)]
    pltpu.make_async_copy(sent, sent, steer_sems.at[0]).wait()
    sent = wall.at[pl.ds(0, 4)]
    pltpu.make_async_copy(sent, sent, steer_sems.at[2]).wait()
    sent = wall.at[pl.ds(0, 3)]
    pltpu.make_async_copy(sent, sent, steer_sems.at[5]).wait()


def channelize(voltages, fir_taps, band_start, steer, station_map, beam_index, calib):
    count = lax.axis_size("chan") * lax.axis_size("sect")
    frames = voltages.shape[2] // 4096
    hbm = pl.BlockSpec(memory_space=pl.ANY)
    vmem = pl.BlockSpec(memory_space=pltpu.VMEM)
    half16 = jnp.bfloat16
    return pl.pallas_call(
        spectra_kernel,
        out_shape=(
            pltpu.VMEM((16, 256, 512), half16),
            pltpu.VMEM((16, 256, 512), half16),
            pltpu.VMEM((1024, 512), half16),
            pltpu.VMEM((512, 512), half16),
        ),
        in_specs=[hbm] * 2 + [vmem] * 7,
        out_specs=(vmem,) * 4,
        scratch_shapes=[
            pltpu.VMEM((2, frames + 6, 2, HALF, 4096), half16),
            pltpu.VMEM((4, 8, 2, HALF, LANES), jnp.float32),
            pltpu.VMEM((BLOCKS * HALF, 2 * LANES), half16),
            pltpu.VMEM((count * PITCH, LANES), jnp.float32),
            pltpu.VMEM((2, count, ROWS, LANES), half16),
            pltpu.VMEM((2, count, ROWS, LANES), half16),
            pltpu.VMEM((512, 1024), half16),
            pltpu.VMEM((2, 512, 1024), jnp.float32),
            pltpu.VMEM((1024, 1024), half16),
            pltpu.VMEM((32, 512), jnp.float32),
            pltpu.VMEM((8, LANES, LANES), half16),
            pltpu.VMEM((512, LANES), half16),
            pltpu.VMEM((8, 512, LANES), half16),
            pltpu.VMEM((LANES, 2 * LANES), half16),
            pltpu.VMEM((1, 512), jnp.int32),
            pltpu.VMEM((512, 1024), half16),
            pltpu.SemaphoreType.DMA((2, 2)),
            pltpu.SemaphoreType.DMA((2, 2)),
            pltpu.SemaphoreType.DMA((2, 2)),
            pltpu.SemaphoreType.DMA((6,)),
        ],
        compiler_params=pltpu.CompilerParams(
            collective_id=0, has_side_effects=True, vmem_limit_bytes=48 * 1024 * 1024
        ),
        name="spectra",
    )(
        voltages,
        steer.reshape(LANES, 1024),
        fir_taps,
        jnp.asarray(twiddles()),
        jnp.asarray(lane_table()),
        band_start.reshape(1, 32),
        station_map.reshape(1, 512),
        beam_index.reshape(1, -1),
        calib.reshape(32, 512),
    )


def product_kernel(
    scale, xt, ct, weights, order, vis, beams, zbuf, wbuf, bbuf, obuf, pbuf, beam_sems, vis_sems
):
    n_b = beams.shape[1]
    tiles = bbuf.shape[0]

    @pl.loop(0, xt.shape[0], unroll=4)
    def _(ch):
        uv = dot(weights[...], ct[ch], NT)
        real = uv[:512, :128] - uv[512:, 128:]
        imag = uv[:512, 128:] + uv[512:, :128]
        both = jnp.concatenate([real, imag], axis=1).astype(jnp.bfloat16)
        rows = pl.ds(pl.multiple_of(ch * 16, 16), 16)
        bbuf[:, rows, :] = both.reshape(tiles, 16, 256)

    line = iota((256, 256), 0)
    source = lax.rem(line, 16) * 16 + line // 16
    move = one_hot(iota((256, 256), 1) == source)

    @pl.loop(0, tiles // 4, unroll=2)
    def _(four):
        for j in range(4):
            tile = four * 4 + j
            out = dot(move, bbuf[tile]).astype(jnp.bfloat16)
            for part in range(2):
                piece = out[:, part * 128 : (part + 1) * 128].reshape(16, 16, 128)
                obuf[part, pl.ds(tile * 16, 16)] = piece

    def put_beams(part):
        return pltpu.make_async_copy(
            obuf.at[part, pl.ds(0, n_b)], beams.at[part], beam_sems.at[part]
        )

    def put_vis(part, g):
        return pltpu.make_async_copy(pbuf.at[part, g % 2], vis.at[part, g], vis_sems.at[part, g % 2])

    for part in range(2):
        put_beams(part).start()

    for g in range(4):
        for a in range(4):
            z = dot(order[...], xt[g * 4 + a], NT).astype(jnp.bfloat16)
            zbuf[:, a * 256 : (a + 1) * 256] = z
            wbuf[:, a * 256 : a * 256 + 128] = z[:, 128:]
            wbuf[:, a * 256 + 128 : (a + 1) * 256] = -z[:, :128]
        for part, left in enumerate((zbuf, wbuf)):
            if g >= 2:
                put_vis(part, g - 2).wait()
            pbuf[part, g % 2] = dot(left[...], zbuf[...], NT) * scale
            put_vis(part, g).start()

    for part in range(2):
        for g in (2, 3):
            put_vis(part, g).wait()
        put_beams(part).wait()


def products(xt, ct, weights, order):
    half16 = jnp.bfloat16
    hbm = pl.BlockSpec(memory_space=pl.ANY)
    vmem = pl.BlockSpec(memory_space=pltpu.VMEM)
    vis, beams = pl.pallas_call(
        functools.partial(product_kernel, 1.0 / 512.0),
        out_shape=(
            jax.ShapeDtypeStruct((2, 4, 512, 512), jnp.float32),
            jax.ShapeDtypeStruct((2, 500, 16, 128), half16),
        ),
        in_specs=[vmem] * 4,
        out_specs=(hbm, hbm),
        scratch_shapes=[
            pltpu.VMEM((512, 1024), half16),
            pltpu.VMEM((512, 1024), half16),
            pltpu.VMEM((32, 256, 256), half16),
            pltpu.VMEM((2, 512, 16, 128), half16),
            pltpu.VMEM((2, 2, 512, 512), jnp.float32),
            pltpu.SemaphoreType.DMA((2,)),
            pltpu.SemaphoreType.DMA((2, 2)),
        ],
        compiler_params=pltpu.CompilerParams(vmem_limit_bytes=40 * 1024 * 1024),
        name="products",
    )(xt, ct, weights, order)
    return vis, jnp.transpose(beams, (0, 2, 1, 3))


def shards(voltages, fir_taps, station_map, band_start, calib, steer, beam_index):
    parts = channelize(
        voltages, fir_taps, band_start, steer, station_map, beam_index, calib
    )
    return products(*parts)


def solution(mesh):
    return jax.shard_map(
        shards,
        mesh=mesh,
        in_specs=(
            P(None, "chan", "sect"),
            P(),
            P(),
            P(),
            P(None, ("chan", "sect"), None),
            P("sect", None, None),
            P(),
        ),
        out_specs=(P(None, ("chan", "sect"), None, None), P(None, ("chan", "sect"), None, None)),
        check_vma=False,
    )
```

```python
import functools
import math

import jax
import jax.numpy as jnp
import numpy as np
from jax import lax
from jax.experimental import pallas as pl
from jax.experimental.pallas import tpu as pltpu
from jax.sharding import PartitionSpec as P

LANES = 128
HALF = 16
BLOCKS = 32
ROWS = 80
PITCH = 81
MESH = pl.DeviceIdType.MESH


def twiddles():
    k = np.arange(BLOCKS)[:, None].astype(np.float64)
    lane = np.arange(LANES)[None, :].astype(np.float64)
    angle = 2.0 * np.pi / 4096.0 * k * lane
    return np.stack([np.cos(angle), -np.sin(angle)]).astype(np.float32)


def lane_table():
    bins = np.arange(LANES)
    angle = 2.0 * np.pi / LANES * (bins[:, None] * bins[None, :] % LANES)
    cosine, sine = np.cos(angle) / 64.0, np.sin(angle) / 64.0
    return np.block([[cosine, sine], [-sine, cosine]]).astype(np.float32)


def cmul_const(re, im, angle):
    c, s = math.cos(angle), math.sin(angle)
    if abs(s) < 1e-12 and c > 0:
        return re, im
    if abs(c) < 1e-12:
        return (im, -re) if s > 0 else (-im, re)
    if abs(abs(c) - abs(s)) < 1e-12 and c > 0 and s > 0:
        return (re + im) * c, (im - re) * c
    if abs(abs(c) - abs(s)) < 1e-12 and c < 0 and s > 0:
        return (im - re) * s, (im + re) * (-s)
    return re * c + im * s, im * c - re * s


def dft4(x):
    (ar, ai), (br, bi), (cr, ci), (dr, di) = x
    pr, pi = ar + cr, ai + ci
    qr, qi = ar - cr, ai - ci
    rr, ri = br + dr, bi + di
    sr, si = br - dr, bi - di
    return [
        (pr + rr, pi + ri),
        (qr + si, qi - sr),
        (pr - rr, pi - ri),
        (qr - si, qi + sr),
    ]


def dft8(x):
    even = dft4(x[0::2])
    odd = dft4(x[1::2])
    odd = [cmul_const(r, i, 2.0 * math.pi * k / 8.0) for k, (r, i) in enumerate(odd)]
    low = [(e[0] + o[0], e[1] + o[1]) for e, o in zip(even, odd)]
    high = [(e[0] - o[0], e[1] - o[1]) for e, o in zip(even, odd)]
    return low + high


NT = (((1,), (1,)), ((), ()))
TN = (((0,), (0,)), ((), ()))


def dot(a, b, dims=(((1,), (0,)), ((), ()))):
    return lax.dot_general(a, b, dims, preferred_element_type=jnp.float32)


def iota(shape, dim):
    return lax.broadcasted_iota(jnp.int32, shape, dim)


def one_hot(found):
    return jnp.where(found, 1.0, 0.0).astype(jnp.bfloat16)


def spectra_kernel(
    volt, steer, taps, tw, lines, bands, smap, beam, calib,
    xt, ct, weights, order,
    vbuf, stage, ybuf, tbuf, sbuf, rbuf, xin, res, ebuf, gains, table, wpart, wall, mat, bidx,
    pick,
    load_sems, send_sems, recv_sems, steer_sems,
):
    me_c = lax.axis_index("chan")
    me_s = lax.axis_index("sect")
    n_c = lax.axis_size("chan")
    n_s = lax.axis_size("sect")
    count = n_c * n_s
    frames = volt.shape[2] // 4096
    core = lax.rem(me_c, 2)
    chip = me_c // 2
    my_x = lax.rem(chip, 2) * 2 + me_s // 4
    my_y = lax.rem(me_s, 4)
    my_z = chip // 2
    mine = my_z * 2 + core

    def load(half, f):
        return pltpu.make_async_copy(
            volt.at[:, pl.ds(half * HALF, HALF), pl.ds(f * 4096, 4096)],
            vbuf.at[half, f + 3],
            load_sems.at[half, f // 8],
        )

    for half in range(2):

        @pl.loop(0, frames)
        def _(f):
            load(half, f).start()

    barrier = pltpu.get_barrier_semaphore()

    @pl.loop(1, count)
    def _(step):
        c = lax.rem(me_c + step // n_s, n_c)
        s = lax.rem(me_s + lax.rem(step, n_s), n_s)
        pl.semaphore_signal(barrier, inc=1, device_id=(c, s), device_id_type=MESH)

    def clear(half, first):
        for pad in range(3):
            vbuf[half, first + pad] = jnp.zeros(vbuf.shape[2:], vbuf.dtype)

    clear(0, 0)

    column = iota((32, LANES), 1)
    spread = one_hot(lax.rem(column, 64) // 2 == iota((32, LANES), 0))
    number = jnp.broadcast_to(bands[...] // 64, (8, 32)).astype(jnp.float32)
    column = iota((8, LANES), 1)
    wanted = dot(number.astype(jnp.bfloat16), spread).astype(jnp.int32) * 2
    wanted = wanted + lax.rem(column, 2) + column // 64 * LANES
    mat[...] = dot(
        one_hot(wanted[:1] == iota((2 * LANES, LANES), 0)), lines[...].astype(jnp.bfloat16), TN
    ).astype(jnp.bfloat16)
    bidx[...] = jnp.full(bidx.shape, -1, jnp.int32)
    bidx[:, : beam.shape[1]] = beam[...]

    def share_table():
        share = steer.at[:, pl.ds(pl.multiple_of(mine * LANES, LANES), LANES)]

        @pl.loop(1, n_s)
        def _(step):
            pltpu.make_async_remote_copy(
                src_ref=share,
                dst_ref=table.at[me_s],
                send_sem=steer_sems.at[0],
                recv_sem=steer_sems.at[1],
                device_id=(me_c, lax.rem(me_s + step, n_s)),
                device_id_type=MESH,
            ).start()

        pltpu.make_async_copy(share, table.at[me_s], steer_sems.at[1]).start()

    def pick_and_share():
        pltpu.make_async_copy(table, table, steer_sems.at[1]).wait()
        entry = jnp.broadcast_to(bidx[...].astype(jnp.float32), (LANES, 512)).T
        entry = entry.astype(jnp.int32)
        for s in range(8):
            found = entry == iota((512, LANES), 1) + s * LANES
            pick[:, s * LANES : (s + 1) * LANES] = one_hot(found)
        wpart[...] = dot(pick[...], table[...].reshape(8 * LANES, LANES)).astype(jnp.bfloat16)

        @pl.loop(1, 4)
        def _(step):
            pltpu.make_async_remote_copy(
                src_ref=wpart,
                dst_ref=wall.at[mine],
                send_sem=steer_sems.at[2],
                recv_sem=steer_sems.at[3],
                device_id=(lax.rem(me_c + step * 4, n_c), me_s),
                device_id_type=MESH,
            ).start()

        pltpu.make_async_remote_copy(
            src_ref=wpart,
            dst_ref=wall.at[mine],
            send_sem=steer_sems.at[2],
            recv_sem=steer_sems.at[4],
            device_id=(me_c + 1 - 2 * core, me_s),
            device_id_type=MESH,
        ).start()
        pltpu.make_async_copy(wpart, wall.at[mine], steer_sems.at[3]).start()

    def pass_on():
        four = wall.at[pl.ds(0, 4)]
        pltpu.make_async_copy(four, four, steer_sems.at[3]).wait()

        @pl.loop(1, 4)
        def _(step):
            other = lax.rem(my_z + step, 4) * 2 + core
            pltpu.make_async_remote_copy(
                src_ref=wall.at[other],
                dst_ref=wall.at[other],
                send_sem=steer_sems.at[5],
                recv_sem=steer_sems.at[4],
                device_id=(me_c + 1 - 2 * core, me_s),
                device_id_type=MESH,
            ).start()

    def one_frame(half, f):
        for q0 in range(8):
            four = []
            for q1 in range(4):
                cols = pl.ds((q0 + 8 * q1) * LANES, LANES)
                parts = []
                for part in range(2):
                    total = None
                    for t in range(4):
                        x = vbuf[half, f + 3 - t, part, :, cols].astype(jnp.float32)
                        term = x * taps[t : t + 1, cols]
                        total = term if total is None else total + term
                    parts.append(total)
                four.append(tuple(parts))
            for ka, (re, im) in enumerate(dft4(four)):
                re, im = cmul_const(re, im, 2.0 * math.pi * q0 * ka / 32.0)
                stage[ka, q0, 0] = re
                stage[ka, q0, 1] = im
        for ka in range(4):
            eight = [(stage[ka, q0, 0], stage[ka, q0, 1]) for q0 in range(8)]
            for kb, (re, im) in enumerate(dft8(eight)):
                k = ka + 4 * kb
                c = tw[0, k : k + 1, :]
                s = tw[1, k : k + 1, :]
                rows = pl.ds(k * HALF, HALF)
                ybuf[rows, :LANES] = (re * c - im * s).astype(jnp.bfloat16)
                ybuf[rows, LANES:] = (re * s + im * c).astype(jnp.bfloat16)
        own = f < frames
        for group in range(4):
            k_hi, kh = group // 2, group % 2
            out = dot(mat[...], ybuf[group * LANES : (group + 1) * LANES, :], NT)
            for part in range(2):
                base = k_hi * 64 * PITCH + jnp.where(
                    own,
                    f // 8 * 48 + kh * 16 + part * 8 + lax.rem(f, 8),
                    32 + kh * 8 + part * 4 + f - frames,
                )
                tbuf[pl.ds(base, 64, stride=PITCH), :] = out[part * 64 : (part + 1) * 64]

    slot = me_s * n_c + me_c

    def message_rows(half, late):
        cut = 48 if half else 32
        return pl.ds(cut, ROWS - cut) if late else pl.ds(0, cut)

    def send_out(half, late):
        rows = message_rows(half, late)

        @pl.loop(0, count // 2)
        def _(step):
            k0 = lax.rem(step, 4)
            k1 = lax.rem(step // 4, 4)
            k2 = step // 16
            x = lax.rem(my_x + k0, 4)
            y = lax.rem(my_y + k0 + k1, 4)
            z = lax.rem(my_z + k0 + k1 + k2, 4)
            for flip in range(2):
                c = (z * 2 + x // 2) * 2 + lax.rem(core + flip, 2)
                s = lax.rem(x, 2) * 4 + y
                dest = c * n_s + s
                first = (lax.rem(dest, 2) * 64 + dest // 2) * PITCH + rows.start
                block = tbuf[pl.ds(first, rows.size), :]
                sbuf[half, dest, rows] = block.astype(jnp.bfloat16)

                def go():
                    pltpu.make_async_remote_copy(
                        src_ref=sbuf.at[half, dest, rows],
                        dst_ref=rbuf.at[half, slot, rows],
                        send_sem=send_sems.at[half, late],
                        recv_sem=recv_sems.at[half, late],
                        device_id=(c, s),
                        device_id_type=MESH,
                    ).start()

                if flip:
                    go()
                else:
                    pl.when(step > 0)(go)

                    @pl.when(step == 0)
                    def _():
                        pltpu.make_async_copy(
                            sbuf.at[half, dest, rows],
                            rbuf.at[half, slot, rows],
                            recv_sems.at[half, late],
                        ).start()

    def arrived(half, late):
        part = vbuf.at[half, pl.ds(3 + 8 * late, 8)]
        pltpu.make_async_copy(part, part, load_sems.at[half, late]).wait()

    arrived(0, 0)

    @pl.loop(0, 8)
    def _(f):
        one_frame(0, f)

    pl.semaphore_wait(barrier, count - 1)
    send_out(0, 0)
    share_table()
    clear(0, frames + 3)
    clear(1, 0)
    clear(1, frames + 3)
    arrived(0, 1)

    @pl.loop(8, frames + 3)
    def _(f):
        one_frame(0, f)

    send_out(0, 1)
    pick_and_share()
    arrived(1, 0)
    arrived(1, 1)

    @pl.loop(0, 11)
    def _(i):
        one_frame(1, jnp.where(i < 8, i, i + 8))

    send_out(1, 0)

    @pl.loop(8, frames)
    def _(f):
        one_frame(1, f)

    send_out(1, 1)
    pass_on()

    rank = iota((512, 512), 1)
    natural = lax.rem(rank // 16, 16) * 32 + rank // 256 * 16 + lax.rem(rank, 16)
    move = one_hot(iota((512, 512), 0) == natural)
    order[...] = dot(one_hot(smap[...] == iota((512, 512), 0)), move).astype(jnp.bfloat16)
    gains[...] = dot(calib[...], order[...])
    line = iota((1024, 1024), 1)
    source = lax.rem(line // 16, 8) * LANES + line // LANES * 16 + lax.rem(line, 16)
    ebuf[...] = one_hot(iota((1024, 1024), 0) == source)
    four = wall.at[pl.ds(0, 4)]
    pltpu.make_async_copy(four, four, steer_sems.at[4]).wait()
    for part in range(2):
        picked = jnp.concatenate([wall[part * 4 + j] for j in range(4)], axis=1)
        weights[part * 512 : (part + 1) * 512, :] = dot(picked, order[...]).astype(jnp.bfloat16)

    row = iota((8, LANES), 0)
    for half in range(2):
        for late in range(2):
            rows = message_rows(half, late)
            pltpu.make_async_copy(
                rbuf.at[half, :, rows], rbuf.at[half, :, rows], recv_sems.at[half, late]
            ).wait()
            if late < 1 - half:
                continue
            for fh in (late,) if half else (0, 1):
                for kh in range(2):
                    for c_hi in range(2):
                        at_row = (kh * 2 + c_hi) * LANES

                        @pl.loop(0, n_s)
                        def _(s):
                            before = jnp.maximum(s - 1, 0)
                            keep = (row < 3) & (s > 0)
                            there = pl.ds(pl.multiple_of(at_row + s * 16, 16), 16)
                            for c_lo in range(8):
                                c = c_hi * 8 + c_lo
                                lanes = slice(c_lo * LANES, (c_lo + 1) * LANES)
                                at = fh * 48 + kh * 16
                                piece = rbuf[half, s * n_c + c, at : at + 16]
                                if fh == 0:
                                    extra = rbuf[half, before * n_c + c, 32:48]
                                    extra = extra.astype(jnp.float32)[kh * 8 : kh * 8 + 8]
                                    extra = jnp.concatenate(
                                        [
                                            jnp.where(keep, extra, 0.0),
                                            jnp.where(keep, pltpu.roll(extra, 4, 0), 0.0),
                                        ],
                                        axis=0,
                                    )
                                    piece = piece.astype(jnp.float32) + extra
                                xin[there, lanes] = piece.astype(jnp.bfloat16)

                res[fh] = dot(xin[...], ebuf[...])

        for kh in range(2):
            for c_hi in range(2):
                cols = slice(half * 256 + c_hi * LANES, half * 256 + (c_hi + 1) * LANES)
                at_row = (kh * 2 + c_hi) * LANES

                @pl.loop(0, n_s)
                def _(s):
                    low = pl.ds(pl.multiple_of(s * 16, 16), 16)
                    high = pl.ds(pl.multiple_of(128 + s * 16, 16), 16)
                    first = pl.ds(pl.multiple_of(at_row + s * 16, 8), 8)
                    second = pl.ds(pl.multiple_of(at_row + s * 16 + 8, 8), 8)
                    for k8 in range(8):
                        ch = kh * 8 + k8
                        lanes = slice(k8 * LANES, (k8 + 1) * LANES)
                        real = jnp.concatenate([res[0, first, lanes], res[1, first, lanes]], axis=0)
                        imag = jnp.concatenate(
                            [res[0, second, lanes], res[1, second, lanes]], axis=0
                        )
                        xt[ch, low, cols] = real.astype(jnp.bfloat16)
                        xt[ch, high, cols] = imag.astype(jnp.bfloat16)
                        g_re = gains[ch : ch + 1, cols]
                        g_im = gains[16 + ch : 17 + ch, cols]
                        ct[ch, low, cols] = (g_re * real - g_im * imag).astype(jnp.bfloat16)
                        ct[ch, high, cols] = (g_re * imag + g_im * real).astype(jnp.bfloat16)

    for half in range(2):
        for late in range(2):
            sent = sbuf.at[half, pl.ds(0, count - 1), message_rows(half, late)]
            pltpu.make_async_copy(sent, sent, send_sems.at[half, late]).wait()
    sent = table.at[pl.ds(0, 7)]
    pltpu.make_async_copy(sent, sent, steer_sems.at[0]).wait()
    sent = wall.at[pl.ds(0, 4)]
    pltpu.make_async_copy(sent, sent, steer_sems.at[2]).wait()
    sent = wall.at[pl.ds(0, 3)]
    pltpu.make_async_copy(sent, sent, steer_sems.at[5]).wait()


def channelize(voltages, fir_taps, band_start, steer, station_map, beam_index, calib):
    count = lax.axis_size("chan") * lax.axis_size("sect")
    frames = voltages.shape[2] // 4096
    hbm = pl.BlockSpec(memory_space=pl.ANY)
    vmem = pl.BlockSpec(memory_space=pltpu.VMEM)
    half16 = jnp.bfloat16
    return pl.pallas_call(
        spectra_kernel,
        out_shape=(
            pltpu.VMEM((16, 256, 512), half16),
            pltpu.VMEM((16, 256, 512), half16),
            pltpu.VMEM((1024, 512), half16),
            pltpu.VMEM((512, 512), half16),
        ),
        in_specs=[hbm] * 2 + [vmem] * 7,
        out_specs=(vmem,) * 4,
        scratch_shapes=[
            pltpu.VMEM((2, frames + 6, 2, HALF, 4096), half16),
            pltpu.VMEM((4, 8, 2, HALF, LANES), jnp.float32),
            pltpu.VMEM((BLOCKS * HALF, 2 * LANES), half16),
            pltpu.VMEM((count * PITCH, LANES), jnp.float32),
            pltpu.VMEM((2, count, ROWS, LANES), half16),
            pltpu.VMEM((2, count, ROWS, LANES), half16),
            pltpu.VMEM((512, 1024), half16),
            pltpu.VMEM((2, 512, 1024), jnp.float32),
            pltpu.VMEM((1024, 1024), half16),
            pltpu.VMEM((32, 512), jnp.float32),
            pltpu.VMEM((8, LANES, LANES), half16),
            pltpu.VMEM((512, LANES), half16),
            pltpu.VMEM((8, 512, LANES), half16),
            pltpu.VMEM((LANES, 2 * LANES), half16),
            pltpu.VMEM((1, 512), jnp.int32),
            pltpu.VMEM((512, 1024), half16),
            pltpu.SemaphoreType.DMA((2, 2)),
            pltpu.SemaphoreType.DMA((2, 2)),
            pltpu.SemaphoreType.DMA((2, 2)),
            pltpu.SemaphoreType.DMA((6,)),
        ],
        compiler_params=pltpu.CompilerParams(
            collective_id=0, has_side_effects=True, vmem_limit_bytes=48 * 1024 * 1024
        ),
        name="spectra",
    )(
        voltages,
        steer.reshape(LANES, 1024),
        fir_taps,
        jnp.asarray(twiddles()),
        jnp.asarray(lane_table()),
        band_start.reshape(1, 32),
        station_map.reshape(1, 512),
        beam_index.reshape(1, -1),
        calib.reshape(32, 512),
    )


def product_kernel(
    scale, xt, ct, weights, order, vis, beams, zbuf, wbuf, bbuf, obuf, pbuf, beam_sems, vis_sems
):
    n_b = beams.shape[1]
    tiles = bbuf.shape[0]

    @pl.loop(0, xt.shape[0], unroll=4)
    def _(ch):
        uv = dot(weights[...], ct[ch], NT)
        real = uv[:512, :128] - uv[512:, 128:]
        imag = uv[:512, 128:] + uv[512:, :128]
        both = jnp.concatenate([real, imag], axis=1).astype(jnp.bfloat16)
        rows = pl.ds(pl.multiple_of(ch * 16, 16), 16)
        bbuf[:, rows, :] = both.reshape(tiles, 16, 256)

    line = iota((256, 256), 0)
    source = lax.rem(line, 16) * 16 + line // 16
    move = one_hot(iota((256, 256), 1) == source)

    @pl.loop(0, tiles // 4, unroll=2)
    def _(four):
        for j in range(4):
            tile = four * 4 + j
            out = dot(move, bbuf[tile]).astype(jnp.bfloat16)
            for part in range(2):
                piece = out[:, part * 128 : (part + 1) * 128].reshape(16, 16, 128)
                obuf[part, pl.ds(tile * 16, 16)] = piece

    def put_beams(part):
        return pltpu.make_async_copy(
            obuf.at[part, pl.ds(0, n_b)], beams.at[part], beam_sems.at[part]
        )

    def put_vis(part, g):
        return pltpu.make_async_copy(pbuf.at[part, g % 2], vis.at[part, g], vis_sems.at[part, g % 2])

    for part in range(2):
        put_beams(part).start()

    for g in range(4):
        for a in range(4):
            z = dot(order[...], xt[g * 4 + a], NT).astype(jnp.bfloat16)
            zbuf[:, a * 256 : (a + 1) * 256] = z
            wbuf[:, a * 256 : a * 256 + 128] = z[:, 128:]
            wbuf[:, a * 256 + 128 : (a + 1) * 256] = -z[:, :128]
        for part, left in enumerate((zbuf, wbuf)):
            if g >= 2:
                put_vis(part, g - 2).wait()
            pbuf[part, g % 2] = dot(left[...], zbuf[...], NT) * scale
            put_vis(part, g).start()

    for part in range(2):
        for g in (2, 3):
            put_vis(part, g).wait()
        put_beams(part).wait()


def products(xt, ct, weights, order):
    half16 = jnp.bfloat16
    hbm = pl.BlockSpec(memory_space=pl.ANY)
    vmem = pl.BlockSpec(memory_space=pltpu.VMEM)
    vis, beams = pl.pallas_call(
        functools.partial(product_kernel, 1.0 / 512.0),
        out_shape=(
            jax.ShapeDtypeStruct((2, 4, 512, 512), jnp.float32),
            jax.ShapeDtypeStruct((2, 500, 16, 128), half16),
        ),
        in_specs=[vmem] * 4,
        out_specs=(hbm, hbm),
        scratch_shapes=[
            pltpu.VMEM((512, 1024), half16),
            pltpu.VMEM((512, 1024), half16),
            pltpu.VMEM((32, 256, 256), half16),
            pltpu.VMEM((2, 512, 16, 128), half16),
            pltpu.VMEM((2, 2, 512, 512), jnp.float32),
            pltpu.SemaphoreType.DMA((2,)),
            pltpu.SemaphoreType.DMA((2, 2)),
        ],
        compiler_params=pltpu.CompilerParams(vmem_limit_bytes=40 * 1024 * 1024),
        name="products",
    )(xt, ct, weights, order)
    return vis, jnp.transpose(beams, (0, 2, 1, 3))


def shards(voltages, fir_taps, station_map, band_start, calib, steer, beam_index):
    parts = channelize(
        voltages, fir_taps, band_start, steer, station_map, beam_index, calib
    )
    return products(*parts)


def solution(mesh):
    return jax.shard_map(
        shards,
        mesh=mesh,
        in_specs=(
            P(None, "chan", "sect"),
            P(),
            P(),
            P(),
            P(None, ("chan", "sect"), None),
            P("sect", None, None),
            P(),
        ),
        out_specs=(P(None, ("chan", "sect"), None, None), P(None, ("chan", "sect"), None, None)),
        check_vma=False,
    )
```

```python
import functools
import math

import jax
import jax.numpy as jnp
import numpy as np
from jax import lax
from jax.experimental import pallas as pl
from jax.experimental.pallas import tpu as pltpu
from jax.sharding import PartitionSpec as P

LANES = 128
HALF = 16
BLOCKS = 32
ROWS = 80
PITCH = 81
MESH = pl.DeviceIdType.MESH


def twiddles():
    k = np.arange(BLOCKS)[:, None].astype(np.float64)
    lane = np.arange(LANES)[None, :].astype(np.float64)
    angle = 2.0 * np.pi / 4096.0 * k * lane
    return np.stack([np.cos(angle), -np.sin(angle)]).astype(np.float32)


def lane_table():
    bins = np.arange(LANES)
    angle = 2.0 * np.pi / LANES * (bins[:, None] * bins[None, :] % LANES)
    cosine, sine = np.cos(angle) / 64.0, np.sin(angle) / 64.0
    return np.block([[cosine, sine], [-sine, cosine]]).astype(np.float32)


def cmul_const(re, im, angle):
    c, s = math.cos(angle), math.sin(angle)
    if abs(s) < 1e-12 and c > 0:
        return re, im
    if abs(c) < 1e-12:
        return (im, -re) if s > 0 else (-im, re)
    if abs(abs(c) - abs(s)) < 1e-12 and c > 0 and s > 0:
        return (re + im) * c, (im - re) * c
    if abs(abs(c) - abs(s)) < 1e-12 and c < 0 and s > 0:
        return (im - re) * s, (im + re) * (-s)
    return re * c + im * s, im * c - re * s


def dft4(x):
    (ar, ai), (br, bi), (cr, ci), (dr, di) = x
    pr, pi = ar + cr, ai + ci
    qr, qi = ar - cr, ai - ci
    rr, ri = br + dr, bi + di
    sr, si = br - dr, bi - di
    return [
        (pr + rr, pi + ri),
        (qr + si, qi - sr),
        (pr - rr, pi - ri),
        (qr - si, qi + sr),
    ]


def dft8(x):
    even = dft4(x[0::2])
    odd = dft4(x[1::2])
    odd = [cmul_const(r, i, 2.0 * math.pi * k / 8.0) for k, (r, i) in enumerate(odd)]
    low = [(e[0] + o[0], e[1] + o[1]) for e, o in zip(even, odd)]
    high = [(e[0] - o[0], e[1] - o[1]) for e, o in zip(even, odd)]
    return low + high


NT = (((1,), (1,)), ((), ()))
TN = (((0,), (0,)), ((), ()))


def dot(a, b, dims=(((1,), (0,)), ((), ()))):
    return lax.dot_general(a, b, dims, preferred_element_type=jnp.float32)


def iota(shape, dim):
    return lax.broadcasted_iota(jnp.int32, shape, dim)


def one_hot(found):
    return jnp.where(found, 1.0, 0.0).astype(jnp.bfloat16)


def spectra_kernel(
    volt, steer, taps, tw, lines, bands, smap, beam, calib,
    xt, ct, weights, order,
    vbuf, stage, ybuf, tbuf, sbuf, rbuf, xin, res, ebuf, gains, table, wpart, wall, mat, bidx,
    pick,
    load_sems, send_sems, recv_sems, steer_sems,
):
    me_c = lax.axis_index("chan")
    me_s = lax.axis_index("sect")
    n_c = lax.axis_size("chan")
    n_s = lax.axis_size("sect")
    count = n_c * n_s
    frames = volt.shape[2] // 4096
    core = lax.rem(me_c, 2)
    chip = me_c // 2
    my_x = lax.rem(chip, 2) * 2 + me_s // 4
    my_y = lax.rem(me_s, 4)
    my_z = chip // 2
    mine = my_z * 2 + core

    def load(half, f):
        return pltpu.make_async_copy(
            volt.at[:, pl.ds(half * HALF, HALF), pl.ds(f * 4096, 4096)],
            vbuf.at[half, f + 3],
            load_sems.at[half, f // 8],
        )

    @pl.loop(0, 8)
    def _(f):
        load(0, f).start()

    barrier = pltpu.get_barrier_semaphore()

    @pl.loop(1, count)
    def _(step):
        c = lax.rem(me_c + step // n_s, n_c)
        s = lax.rem(me_s + lax.rem(step, n_s), n_s)
        pl.semaphore_signal(barrier, inc=1, device_id=(c, s), device_id_type=MESH)

    @pl.loop(8, frames)
    def _(f):
        load(0, f).start()

    @pl.loop(0, frames)
    def _(f):
        load(1, f).start()

    def clear(half, first):
        for pad in range(4 if first else 3):
            vbuf[half, first + pad] = jnp.zeros(vbuf.shape[2:], vbuf.dtype)

    clear(0, 0)

    column = iota((32, LANES), 1)
    spread = one_hot(lax.rem(column, 64) // 2 == iota((32, LANES), 0))
    number = jnp.broadcast_to(bands[...] // 64, (8, 32)).astype(jnp.float32)
    column = iota((8, LANES), 1)
    wanted = dot(number.astype(jnp.bfloat16), spread).astype(jnp.int32) * 2
    wanted = wanted + lax.rem(column, 2) + column // 64 * LANES
    mat[...] = dot(
        one_hot(wanted[:1] == iota((2 * LANES, LANES), 0)), lines[...].astype(jnp.bfloat16), TN
    ).astype(jnp.bfloat16)
    bidx[...] = jnp.full(bidx.shape, -1, jnp.int32)
    bidx[:, : beam.shape[1]] = beam[...]

    def share_table():
        share = steer.at[:, pl.ds(pl.multiple_of(mine * LANES, LANES), LANES)]

        @pl.loop(1, n_s)
        def _(step):
            pltpu.make_async_remote_copy(
                src_ref=share,
                dst_ref=table.at[me_s],
                send_sem=steer_sems.at[0],
                recv_sem=steer_sems.at[1],
                device_id=(me_c, lax.rem(me_s + step, n_s)),
                device_id_type=MESH,
            ).start()

        pltpu.make_async_copy(share, table.at[me_s], steer_sems.at[1]).start()

    def pick_and_share():
        pltpu.make_async_copy(table, table, steer_sems.at[1]).wait()
        entry = jnp.broadcast_to(bidx[...].astype(jnp.float32), (LANES, 512)).T
        entry = entry.astype(jnp.int32)
        for s in range(8):
            found = entry == iota((512, LANES), 1) + s * LANES
            pick[:, s * LANES : (s + 1) * LANES] = one_hot(found)
        wpart[...] = dot(pick[...], table[...].reshape(8 * LANES, LANES)).astype(jnp.bfloat16)

        @pl.loop(1, 4)
        def _(step):
            pltpu.make_async_remote_copy(
                src_ref=wpart,
                dst_ref=wall.at[mine],
                send_sem=steer_sems.at[2],
                recv_sem=steer_sems.at[3],
                device_id=(lax.rem(me_c + step * 4, n_c), me_s),
                device_id_type=MESH,
            ).start()

        pltpu.make_async_remote_copy(
            src_ref=wpart,
            dst_ref=wall.at[mine],
            send_sem=steer_sems.at[2],
            recv_sem=steer_sems.at[4],
            device_id=(me_c + 1 - 2 * core, me_s),
            device_id_type=MESH,
        ).start()
        pltpu.make_async_copy(wpart, wall.at[mine], steer_sems.at[3]).start()

    def pass_on():
        four = wall.at[pl.ds(0, 4)]
        pltpu.make_async_copy(four, four, steer_sems.at[3]).wait()

        @pl.loop(1, 4)
        def _(step):
            other = lax.rem(my_z + step, 4) * 2 + core
            pltpu.make_async_remote_copy(
                src_ref=wall.at[other],
                dst_ref=wall.at[other],
                send_sem=steer_sems.at[5],
                recv_sem=steer_sems.at[4],
                device_id=(me_c + 1 - 2 * core, me_s),
                device_id_type=MESH,
            ).start()

    def frame_pair(half, f0):
        for q0 in range(8):
            four = ([], [])
            for q1 in range(4):
                cols = pl.ds((q0 + 8 * q1) * LANES, LANES)
                tap = [taps[t : t + 1, cols] for t in range(4)]
                parts = ([], [])
                for part in range(2):
                    x = [
                        vbuf[half, f0 + 4 - t, part, :, cols].astype(jnp.float32) for t in range(5)
                    ]
                    for which in range(2):
                        total = None
                        for t in range(4):
                            term = x[t + 1 - which] * tap[t]
                            total = term if total is None else total + term
                        parts[which].append(total)
                for which in range(2):
                    four[which].append(tuple(parts[which]))
            for which in range(2):
                for ka, (re, im) in enumerate(dft4(four[which])):
                    re, im = cmul_const(re, im, 2.0 * math.pi * q0 * ka / 32.0)
                    stage[which, ka, q0, 0] = re
                    stage[which, ka, q0, 1] = im
        for which in range(2):
            finish(f0 + which, which)

    def finish(f, which):
        for ka in range(4):
            eight = [(stage[which, ka, q0, 0], stage[which, ka, q0, 1]) for q0 in range(8)]
            for kb, (re, im) in enumerate(dft8(eight)):
                k = ka + 4 * kb
                c = tw[0, k : k + 1, :]
                s = tw[1, k : k + 1, :]
                rows = pl.ds(k * HALF, HALF)
                ybuf[rows, :LANES] = (re * c - im * s).astype(jnp.bfloat16)
                ybuf[rows, LANES:] = (re * s + im * c).astype(jnp.bfloat16)
        own = f < frames
        for group in range(4):
            k_hi, kh = group // 2, group % 2
            out = dot(mat[...], ybuf[group * LANES : (group + 1) * LANES, :], NT)
            for part in range(2):
                base = k_hi * 64 * PITCH + jnp.where(
                    own,
                    f // 8 * 48 + kh * 16 + part * 8 + lax.rem(f, 8),
                    32 + kh * 8 + part * 4 + f - frames,
                )
                tbuf[pl.ds(base, 64, stride=PITCH), :] = out[part * 64 : (part + 1) * 64]

    slot = me_s * n_c + me_c

    def message_rows(half, late):
        cut = 48 if half else 32
        return pl.ds(cut, ROWS - cut) if late else pl.ds(0, cut)

    def send_out(half, late):
        rows = message_rows(half, late)

        @pl.loop(0, count // 2)
        def _(step):
            k0 = lax.rem(step, 4)
            k1 = lax.rem(step // 4, 4)
            k2 = step // 16
            x = lax.rem(my_x + k0, 4)
            y = lax.rem(my_y + k0 + k1, 4)
            z = lax.rem(my_z + k0 + k1 + k2, 4)
            for flip in range(2):
                c = (z * 2 + x // 2) * 2 + lax.rem(core + flip, 2)
                s = lax.rem(x, 2) * 4 + y
                dest = c * n_s + s
                first = (lax.rem(dest, 2) * 64 + dest // 2) * PITCH + rows.start
                block = tbuf[pl.ds(first, rows.size), :]
                sbuf[half, dest, rows] = block.astype(jnp.bfloat16)

                def go():
                    pltpu.make_async_remote_copy(
                        src_ref=sbuf.at[half, dest, rows],
                        dst_ref=rbuf.at[half, slot, rows],
                        send_sem=send_sems.at[half, late],
                        recv_sem=recv_sems.at[half, late],
                        device_id=(c, s),
                        device_id_type=MESH,
                    ).start()

                if flip:
                    go()
                else:
                    pl.when(step > 0)(go)

                    @pl.when(step == 0)
                    def _():
                        pltpu.make_async_copy(
                            sbuf.at[half, dest, rows],
                            rbuf.at[half, slot, rows],
                            recv_sems.at[half, late],
                        ).start()

    def arrived(half, late):
        part = vbuf.at[half, pl.ds(3 + 8 * late, 8)]
        pltpu.make_async_copy(part, part, load_sems.at[half, late]).wait()

    arrived(0, 0)

    @pl.loop(0, 4)
    def _(i):
        frame_pair(0, 2 * i)

    pl.semaphore_wait(barrier, count - 1)
    send_out(0, 0)
    share_table()
    clear(0, frames + 3)
    clear(1, 0)
    clear(1, frames + 3)
    arrived(0, 1)

    @pl.loop(4, 10)
    def _(i):
        frame_pair(0, 2 * i)

    send_out(0, 1)
    pick_and_share()
    arrived(1, 0)
    arrived(1, 1)

    @pl.loop(0, 6)
    def _(i):
        frame_pair(1, 2 * jnp.where(i < 4, i, i + 4))

    send_out(1, 0)

    @pl.loop(4, 8)
    def _(i):
        frame_pair(1, 2 * i)

    send_out(1, 1)
    pass_on()

    rank = iota((512, 512), 1)
    natural = lax.rem(rank // 16, 16) * 32 + rank // 256 * 16 + lax.rem(rank, 16)
    move = one_hot(iota((512, 512), 0) == natural)
    order[...] = dot(one_hot(smap[...] == iota((512, 512), 0)), move).astype(jnp.bfloat16)
    gains[...] = dot(calib[...], order[...])
    line = iota((1024, 1024), 1)
    source = lax.rem(line // 16, 8) * LANES + line // LANES * 16 + lax.rem(line, 16)
    ebuf[...] = one_hot(iota((1024, 1024), 0) == source)
    four = wall.at[pl.ds(0, 4)]
    pltpu.make_async_copy(four, four, steer_sems.at[4]).wait()
    for part in range(2):
        picked = jnp.concatenate([wall[part * 4 + j] for j in range(4)], axis=1)
        weights[part * 512 : (part + 1) * 512, :] = dot(picked, order[...]).astype(jnp.bfloat16)

    row = iota((8, LANES), 0)
    for half in range(2):
        for late in range(2):
            rows = message_rows(half, late)
            pltpu.make_async_copy(
                rbuf.at[half, :, rows], rbuf.at[half, :, rows], recv_sems.at[half, late]
            ).wait()
            if late < 1 - half:
                continue
            for fh in (late,) if half else (0, 1):
                for kh in range(2):
                    for c_hi in range(2):
                        at_row = (kh * 2 + c_hi) * LANES

                        @pl.loop(0, n_s)
                        def _(s):
                            before = jnp.maximum(s - 1, 0)
                            keep = (row < 3) & (s > 0)
                            there = pl.ds(pl.multiple_of(at_row + s * 16, 16), 16)
                            for c_lo in range(8):
                                c = c_hi * 8 + c_lo
                                lanes = slice(c_lo * LANES, (c_lo + 1) * LANES)
                                at = fh * 48 + kh * 16
                                piece = rbuf[half, s * n_c + c, at : at + 16]
                                if fh == 0:
                                    extra = rbuf[half, before * n_c + c, 32:48]
                                    extra = extra.astype(jnp.float32)[kh * 8 : kh * 8 + 8]
                                    extra = jnp.concatenate(
                                        [
                                            jnp.where(keep, extra, 0.0),
                                            jnp.where(keep, pltpu.roll(extra, 4, 0), 0.0),
                                        ],
                                        axis=0,
                                    )
                                    piece = piece.astype(jnp.float32) + extra
                                xin[there, lanes] = piece.astype(jnp.bfloat16)

                res[fh] = dot(xin[...], ebuf[...])

        for kh in range(2):
            for c_hi in range(2):
                cols = slice(half * 256 + c_hi * LANES, half * 256 + (c_hi + 1) * LANES)
                at_row = (kh * 2 + c_hi) * LANES

                @pl.loop(0, n_s)
                def _(s):
                    low = pl.ds(pl.multiple_of(s * 16, 16), 16)
                    high = pl.ds(pl.multiple_of(128 + s * 16, 16), 16)
                    first = pl.ds(pl.multiple_of(at_row + s * 16, 8), 8)
                    second = pl.ds(pl.multiple_of(at_row + s * 16 + 8, 8), 8)
                    for k8 in range(8):
                        ch = kh * 8 + k8
                        lanes = slice(k8 * LANES, (k8 + 1) * LANES)
                        real = jnp.concatenate([res[0, first, lanes], res[1, first, lanes]], axis=0)
                        imag = jnp.concatenate(
                            [res[0, second, lanes], res[1, second, lanes]], axis=0
                        )
                        xt[ch, low, cols] = real.astype(jnp.bfloat16)
                        xt[ch, high, cols] = imag.astype(jnp.bfloat16)
                        g_re = gains[ch : ch + 1, cols]
                        g_im = gains[16 + ch : 17 + ch, cols]
                        ct[ch, low, cols] = (g_re * real - g_im * imag).astype(jnp.bfloat16)
                        ct[ch, high, cols] = (g_re * imag + g_im * real).astype(jnp.bfloat16)

    for half in range(2):
        for late in range(2):
            sent = sbuf.at[half, pl.ds(0, count - 1), message_rows(half, late)]
            pltpu.make_async_copy(sent, sent, send_sems.at[half, late]).wait()
    sent = table.at[pl.ds(0, 7)]
    pltpu.make_async_copy(sent, sent, steer_sems.at[0]).wait()
    sent = wall.at[pl.ds(0, 4)]
    pltpu.make_async_copy(sent, sent, steer_sems.at[2]).wait()
    sent = wall.at[pl.ds(0, 3)]
    pltpu.make_async_copy(sent, sent, steer_sems.at[5]).wait()


def channelize(voltages, fir_taps, band_start, steer, station_map, beam_index, calib):
    count = lax.axis_size("chan") * lax.axis_size("sect")
    frames = voltages.shape[2] // 4096
    hbm = pl.BlockSpec(memory_space=pl.ANY)
    vmem = pl.BlockSpec(memory_space=pltpu.VMEM)
    half16 = jnp.bfloat16
    return pl.pallas_call(
        spectra_kernel,
        out_shape=(
            pltpu.VMEM((16, 256, 512), half16),
            pltpu.VMEM((16, 256, 512), half16),
            pltpu.VMEM((1024, 512), half16),
            pltpu.VMEM((512, 512), half16),
        ),
        in_specs=[hbm] * 2 + [vmem] * 7,
        out_specs=(vmem,) * 4,
        scratch_shapes=[
            pltpu.VMEM((2, frames + 7, 2, HALF, 4096), half16),
            pltpu.VMEM((2, 4, 8, 2, HALF, LANES), jnp.float32),
            pltpu.VMEM((BLOCKS * HALF, 2 * LANES), half16),
            pltpu.VMEM((count * PITCH, LANES), jnp.float32),
            pltpu.VMEM((2, count, ROWS, LANES), half16),
            pltpu.VMEM((2, count, ROWS, LANES), half16),
            pltpu.VMEM((512, 1024), half16),
            pltpu.VMEM((2, 512, 1024), jnp.float32),
            pltpu.VMEM((1024, 1024), half16),
            pltpu.VMEM((32, 512), jnp.float32),
            pltpu.VMEM((8, LANES, LANES), half16),
            pltpu.VMEM((512, LANES), half16),
            pltpu.VMEM((8, 512, LANES), half16),
            pltpu.VMEM((LANES, 2 * LANES), half16),
            pltpu.VMEM((1, 512), jnp.int32),
            pltpu.VMEM((512, 1024), half16),
            pltpu.SemaphoreType.DMA((2, 2)),
            pltpu.SemaphoreType.DMA((2, 2)),
            pltpu.SemaphoreType.DMA((2, 2)),
            pltpu.SemaphoreType.DMA((6,)),
        ],
        compiler_params=pltpu.CompilerParams(
            collective_id=0, has_side_effects=True, vmem_limit_bytes=48 * 1024 * 1024
        ),
        name="spectra",
    )(
        voltages,
        steer.reshape(LANES, 1024),
        fir_taps,
        jnp.asarray(twiddles()),
        jnp.asarray(lane_table()),
        band_start.reshape(1, 32),
        station_map.reshape(1, 512),
        beam_index.reshape(1, -1),
        calib.reshape(32, 512),
    )


def product_kernel(
    scale, xt, ct, weights, order, vis, beams, zbuf, wbuf, bbuf, obuf, pbuf, beam_sems, vis_sems
):
    n_b = beams.shape[1]
    tiles = bbuf.shape[0]

    @pl.loop(0, xt.shape[0], unroll=8)
    def _(ch):
        uv = dot(weights[...], ct[ch], NT)
        real = uv[:512, :128] - uv[512:, 128:]
        imag = uv[:512, 128:] + uv[512:, :128]
        both = jnp.concatenate([real, imag], axis=1).astype(jnp.bfloat16)
        rows = pl.ds(pl.multiple_of(ch * 16, 16), 16)
        bbuf[:, rows, :] = both.reshape(tiles, 16, 256)

    line = iota((256, 256), 0)
    source = lax.rem(line, 16) * 16 + line // 16
    move = one_hot(iota((256, 256), 1) == source)

    @pl.loop(0, tiles // 4, unroll=4)
    def _(four):
        for j in range(4):
            tile = four * 4 + j
            out = dot(move, bbuf[tile]).astype(jnp.bfloat16)
            for part in range(2):
                piece = out[:, part * 128 : (part + 1) * 128].reshape(16, 16, 128)
                obuf[part, pl.ds(tile * 16, 16)] = piece

    def put_beams(part):
        return pltpu.make_async_copy(
            obuf.at[part, pl.ds(0, n_b)], beams.at[part], beam_sems.at[part]
        )

    def put_vis(part, g):
        return pltpu.make_async_copy(pbuf.at[part, g % 2], vis.at[part, g], vis_sems.at[part, g % 2])

    for part in range(2):
        put_beams(part).start()

    for g in range(4):
        for a in range(4):
            z = dot(order[...], xt[g * 4 + a], NT).astype(jnp.bfloat16)
            zbuf[:, a * 256 : (a + 1) * 256] = z
            wbuf[:, a * 256 : a * 256 + 128] = z[:, 128:]
            wbuf[:, a * 256 + 128 : (a + 1) * 256] = -z[:, :128]
        for part, left in enumerate((zbuf, wbuf)):
            if g >= 2:
                put_vis(part, g - 2).wait()
            pbuf[part, g % 2] = dot(left[...], zbuf[...], NT) * scale
            put_vis(part, g).start()

    for part in range(2):
        for g in (2, 3):
            put_vis(part, g).wait()
        put_beams(part).wait()


def products(xt, ct, weights, order):
    half16 = jnp.bfloat16
    hbm = pl.BlockSpec(memory_space=pl.ANY)
    vmem = pl.BlockSpec(memory_space=pltpu.VMEM)
    vis, beams = pl.pallas_call(
        functools.partial(product_kernel, 1.0 / 512.0),
        out_shape=(
            jax.ShapeDtypeStruct((2, 4, 512, 512), jnp.float32),
            jax.ShapeDtypeStruct((2, 500, 16, 128), half16),
        ),
        in_specs=[vmem] * 4,
        out_specs=(hbm, hbm),
        scratch_shapes=[
            pltpu.VMEM((512, 1024), half16),
            pltpu.VMEM((512, 1024), half16),
            pltpu.VMEM((32, 256, 256), half16),
            pltpu.VMEM((2, 512, 16, 128), half16),
            pltpu.VMEM((2, 2, 512, 512), jnp.float32),
            pltpu.SemaphoreType.DMA((2,)),
            pltpu.SemaphoreType.DMA((2, 2)),
        ],
        compiler_params=pltpu.CompilerParams(vmem_limit_bytes=40 * 1024 * 1024),
        name="products",
    )(xt, ct, weights, order)
    return vis, jnp.transpose(beams, (0, 2, 1, 3))


def shards(voltages, fir_taps, station_map, band_start, calib, steer, beam_index):
    parts = channelize(
        voltages, fir_taps, band_start, steer, station_map, beam_index, calib
    )
    return products(*parts)


def solution(mesh):
    return jax.shard_map(
        shards,
        mesh=mesh,
        in_specs=(
            P(None, "chan", "sect"),
            P(),
            P(),
            P(),
            P(None, ("chan", "sect"), None),
            P("sect", None, None),
            P(),
        ),
        out_specs=(P(None, ("chan", "sect"), None, None), P(None, ("chan", "sect"), None, None)),
        check_vma=False,
    )
```

```python
import functools
import math

import jax
import jax.numpy as jnp
import numpy as np
from jax import lax
from jax.experimental import pallas as pl
from jax.experimental.pallas import tpu as pltpu
from jax.sharding import PartitionSpec as P

LANES = 128
HALF = 16
BLOCKS = 32
ROWS = 80
PITCH = 81
MESH = pl.DeviceIdType.MESH


def twiddles():
    k = np.arange(BLOCKS)[:, None].astype(np.float64)
    lane = np.arange(LANES)[None, :].astype(np.float64)
    angle = 2.0 * np.pi / 4096.0 * k * lane
    return np.stack([np.cos(angle), -np.sin(angle)]).astype(np.float32)


def lane_table():
    bins = np.arange(LANES)
    angle = 2.0 * np.pi / LANES * (bins[:, None] * bins[None, :] % LANES)
    cosine, sine = np.cos(angle) / 64.0, np.sin(angle) / 64.0
    return np.block([[cosine, sine], [-sine, cosine]]).astype(np.float32)


def cmul_const(re, im, angle):
    c, s = math.cos(angle), math.sin(angle)
    if abs(s) < 1e-12 and c > 0:
        return re, im
    if abs(c) < 1e-12:
        return (im, -re) if s > 0 else (-im, re)
    if abs(abs(c) - abs(s)) < 1e-12 and c > 0 and s > 0:
        return (re + im) * c, (im - re) * c
    if abs(abs(c) - abs(s)) < 1e-12 and c < 0 and s > 0:
        return (im - re) * s, (im + re) * (-s)
    return re * c + im * s, im * c - re * s


def dft4(x):
    (ar, ai), (br, bi), (cr, ci), (dr, di) = x
    pr, pi = ar + cr, ai + ci
    qr, qi = ar - cr, ai - ci
    rr, ri = br + dr, bi + di
    sr, si = br - dr, bi - di
    return [
        (pr + rr, pi + ri),
        (qr + si, qi - sr),
        (pr - rr, pi - ri),
        (qr - si, qi + sr),
    ]


def dft8(x):
    even = dft4(x[0::2])
    odd = dft4(x[1::2])
    odd = [cmul_const(r, i, 2.0 * math.pi * k / 8.0) for k, (r, i) in enumerate(odd)]
    low = [(e[0] + o[0], e[1] + o[1]) for e, o in zip(even, odd)]
    high = [(e[0] - o[0], e[1] - o[1]) for e, o in zip(even, odd)]
    return low + high


NT = (((1,), (1,)), ((), ()))
TN = (((0,), (0,)), ((), ()))


def dot(a, b, dims=(((1,), (0,)), ((), ()))):
    return lax.dot_general(a, b, dims, preferred_element_type=jnp.float32)


def iota(shape, dim):
    return lax.broadcasted_iota(jnp.int32, shape, dim)


def one_hot(found):
    return jnp.where(found, 1.0, 0.0).astype(jnp.bfloat16)


def spectra_kernel(
    volt, steer, taps, tw, lines, bands, smap, beam, calib,
    xt, ct, weights, order,
    vbuf, stage, ybuf, tbuf, sbuf, rbuf, xin, res, ebuf, gains, table, wpart, wall, mat, bidx,
    pick, shares,
    load_sems, send_sems, recv_sems, steer_sems,
):
    me_c = lax.axis_index("chan")
    me_s = lax.axis_index("sect")
    n_c = lax.axis_size("chan")
    n_s = lax.axis_size("sect")
    count = n_c * n_s
    frames = volt.shape[2] // 4096
    core = lax.rem(me_c, 2)
    chip = me_c // 2
    my_x = lax.rem(chip, 2) * 2 + me_s // 4
    my_y = lax.rem(me_s, 4)
    my_z = chip // 2
    mine = my_z * 2 + core

    def load(half, f):
        return pltpu.make_async_copy(
            volt.at[:, pl.ds(half * HALF, HALF), pl.ds(f * 4096, 4096)],
            vbuf.at[half, f + 3],
            load_sems.at[half, f // 8],
        )

    @pl.loop(0, 8)
    def _(f):
        load(0, f).start()

    barrier = pltpu.get_barrier_semaphore()

    @pl.loop(1, count)
    def _(step):
        c = lax.rem(me_c + step // n_s, n_c)
        s = lax.rem(me_s + lax.rem(step, n_s), n_s)
        pl.semaphore_signal(barrier, inc=1, device_id=(c, s), device_id_type=MESH)

    @pl.loop(8, frames)
    def _(f):
        load(0, f).start()

    @pl.loop(0, frames)
    def _(f):
        load(1, f).start()

    def clear(half, first):
        for pad in range(4 if first else 3):
            vbuf[half, first + pad] = jnp.zeros(vbuf.shape[2:], vbuf.dtype)

    clear(0, 0)

    column = iota((32, LANES), 1)
    spread = one_hot(lax.rem(column, 64) // 2 == iota((32, LANES), 0))
    number = jnp.broadcast_to(bands[...] // 64, (8, 32)).astype(jnp.float32)
    column = iota((8, LANES), 1)
    wanted = dot(number.astype(jnp.bfloat16), spread).astype(jnp.int32) * 2
    wanted = wanted + lax.rem(column, 2) + column // 64 * LANES
    mat[...] = dot(
        one_hot(wanted[:1] == iota((2 * LANES, LANES), 0)), lines[...].astype(jnp.bfloat16), TN
    ).astype(jnp.bfloat16)
    bidx[...] = jnp.full(bidx.shape, -1, jnp.int32)
    bidx[:, : beam.shape[1]] = beam[...]

    def share_table():
        for part in range(2):
            for j in range(4):
                shares[part * 4 + j] = steer[:, part, j * LANES : (j + 1) * LANES]
        share = shares.at[mine]

        @pl.loop(1, n_s)
        def _(step):
            pltpu.make_async_remote_copy(
                src_ref=share,
                dst_ref=table.at[me_s],
                send_sem=steer_sems.at[0],
                recv_sem=steer_sems.at[1],
                device_id=(me_c, lax.rem(me_s + step, n_s)),
                device_id_type=MESH,
            ).start()

        pltpu.make_async_copy(share, table.at[me_s], steer_sems.at[1]).start()

    def pick_and_share():
        pltpu.make_async_copy(table, table, steer_sems.at[1]).wait()
        entry = jnp.broadcast_to(bidx[...].astype(jnp.float32), (LANES, 512)).T
        entry = entry.astype(jnp.int32)
        for s in range(8):
            found = entry == iota((512, LANES), 1) + s * LANES
            pick[:, s * LANES : (s + 1) * LANES] = one_hot(found)
        wpart[...] = dot(pick[...], table[...].reshape(8 * LANES, LANES)).astype(jnp.bfloat16)

        @pl.loop(1, 4)
        def _(step):
            pltpu.make_async_remote_copy(
                src_ref=wpart,
                dst_ref=wall.at[mine],
                send_sem=steer_sems.at[2],
                recv_sem=steer_sems.at[3],
                device_id=(lax.rem(me_c + step * 4, n_c), me_s),
                device_id_type=MESH,
            ).start()

        pltpu.make_async_remote_copy(
            src_ref=wpart,
            dst_ref=wall.at[mine],
            send_sem=steer_sems.at[2],
            recv_sem=steer_sems.at[4],
            device_id=(me_c + 1 - 2 * core, me_s),
            device_id_type=MESH,
        ).start()
        pltpu.make_async_copy(wpart, wall.at[mine], steer_sems.at[3]).start()

    def pass_on():
        four = wall.at[pl.ds(0, 4)]
        pltpu.make_async_copy(four, four, steer_sems.at[3]).wait()

        @pl.loop(1, 4)
        def _(step):
            other = lax.rem(my_z + step, 4) * 2 + core
            pltpu.make_async_remote_copy(
                src_ref=wall.at[other],
                dst_ref=wall.at[other],
                send_sem=steer_sems.at[5],
                recv_sem=steer_sems.at[4],
                device_id=(me_c + 1 - 2 * core, me_s),
                device_id_type=MESH,
            ).start()

    def frame_pair(half, f0):
        for q0 in range(8):
            four = ([], [])
            for q1 in range(4):
                cols = pl.ds((q0 + 8 * q1) * LANES, LANES)
                tap = [taps[t : t + 1, cols] for t in range(4)]
                parts = ([], [])
                for part in range(2):
                    x = [
                        vbuf[half, f0 + 4 - t, part, :, cols].astype(jnp.float32) for t in range(5)
                    ]
                    for which in range(2):
                        total = None
                        for t in range(4):
                            term = x[t + 1 - which] * tap[t]
                            total = term if total is None else total + term
                        parts[which].append(total)
                for which in range(2):
                    four[which].append(tuple(parts[which]))
            for which in range(2):
                for ka, (re, im) in enumerate(dft4(four[which])):
                    re, im = cmul_const(re, im, 2.0 * math.pi * q0 * ka / 32.0)
                    stage[which, ka, q0, 0] = re
                    stage[which, ka, q0, 1] = im
        for which in range(2):
            finish(f0 + which, which)

    def finish(f, which):
        for ka in range(4):
            eight = [(stage[which, ka, q0, 0], stage[which, ka, q0, 1]) for q0 in range(8)]
            for kb, (re, im) in enumerate(dft8(eight)):
                k = ka + 4 * kb
                c = tw[0, k : k + 1, :]
                s = tw[1, k : k + 1, :]
                rows = pl.ds(k * HALF, HALF)
                ybuf[rows, :LANES] = (re * c - im * s).astype(jnp.bfloat16)
                ybuf[rows, LANES:] = (re * s + im * c).astype(jnp.bfloat16)
        own = f < frames
        for group in range(4):
            k_hi, kh = group // 2, group % 2
            out = dot(mat[...], ybuf[group * LANES : (group + 1) * LANES, :], NT)
            for part in range(2):
                base = k_hi * 64 * PITCH + jnp.where(
                    own,
                    f // 8 * 48 + kh * 16 + part * 8 + lax.rem(f, 8),
                    32 + kh * 8 + part * 4 + f - frames,
                )
                tbuf[pl.ds(base, 64, stride=PITCH), :] = out[part * 64 : (part + 1) * 64]

    slot = me_s * n_c + me_c

    def message_rows(half, late):
        cut = 48 if half else 32
        return pl.ds(cut, ROWS - cut) if late else pl.ds(0, cut)

    def send_out(half, late):
        rows = message_rows(half, late)

        @pl.loop(0, count // 2)
        def _(step):
            k0 = lax.rem(step, 4)
            k1 = lax.rem(step // 4, 4)
            k2 = step // 16
            x = lax.rem(my_x + k0, 4)
            y = lax.rem(my_y + k0 + k1, 4)
            z = lax.rem(my_z + k0 + k1 + k2, 4)
            for flip in range(2):
                c = (z * 2 + x // 2) * 2 + lax.rem(core + flip, 2)
                s = lax.rem(x, 2) * 4 + y
                dest = c * n_s + s
                first = (lax.rem(dest, 2) * 64 + dest // 2) * PITCH + rows.start
                block = tbuf[pl.ds(first, rows.size), :]
                sbuf[half, dest, rows] = block.astype(jnp.bfloat16)

                def go():
                    pltpu.make_async_remote_copy(
                        src_ref=sbuf.at[half, dest, rows],
                        dst_ref=rbuf.at[half, slot, rows],
                        send_sem=send_sems.at[half, late],
                        recv_sem=recv_sems.at[half, late],
                        device_id=(c, s),
                        device_id_type=MESH,
                    ).start()

                if flip:
                    go()
                else:
                    pl.when(step > 0)(go)

                    @pl.when(step == 0)
                    def _():
                        pltpu.make_async_copy(
                            sbuf.at[half, dest, rows],
                            rbuf.at[half, slot, rows],
                            recv_sems.at[half, late],
                        ).start()

    def arrived(half, late):
        part = vbuf.at[half, pl.ds(3 + 8 * late, 8)]
        pltpu.make_async_copy(part, part, load_sems.at[half, late]).wait()

    arrived(0, 0)

    @pl.loop(0, 4)
    def _(i):
        frame_pair(0, 2 * i)

    pl.semaphore_wait(barrier, count - 1)
    send_out(0, 0)
    share_table()
    clear(0, frames + 3)
    clear(1, 0)
    clear(1, frames + 3)
    arrived(0, 1)

    @pl.loop(4, 10)
    def _(i):
        frame_pair(0, 2 * i)

    send_out(0, 1)
    pick_and_share()
    arrived(1, 0)
    arrived(1, 1)

    @pl.loop(0, 6)
    def _(i):
        frame_pair(1, 2 * jnp.where(i < 4, i, i + 4))

    send_out(1, 0)

    @pl.loop(4, 8)
    def _(i):
        frame_pair(1, 2 * i)

    send_out(1, 1)
    pass_on()

    rank = iota((512, 512), 1)
    natural = lax.rem(rank // 16, 16) * 32 + rank // 256 * 16 + lax.rem(rank, 16)
    move = one_hot(iota((512, 512), 0) == natural)
    order[...] = dot(one_hot(smap[...] == iota((512, 512), 0)), move).astype(jnp.bfloat16)
    gains[...] = dot(calib[...], order[...])
    line = iota((1024, 1024), 1)
    source = lax.rem(line // 16, 8) * LANES + line // LANES * 16 + lax.rem(line, 16)
    ebuf[...] = one_hot(iota((1024, 1024), 0) == source)
    four = wall.at[pl.ds(0, 4)]
    pltpu.make_async_copy(four, four, steer_sems.at[4]).wait()
    for part in range(2):
        picked = jnp.concatenate([wall[part * 4 + j] for j in range(4)], axis=1)
        weights[part * 512 : (part + 1) * 512, :] = dot(picked, order[...]).astype(jnp.bfloat16)

    row = iota((8, LANES), 0)
    for half in range(2):
        for late in range(2):
            rows = message_rows(half, late)
            pltpu.make_async_copy(
                rbuf.at[half, :, rows], rbuf.at[half, :, rows], recv_sems.at[half, late]
            ).wait()
            if late < 1 - half:
                continue
            for fh in (late,) if half else (0, 1):
                for kh in range(2):
                    for c_hi in range(2):
                        at_row = (kh * 2 + c_hi) * LANES

                        @pl.loop(0, n_s)
                        def _(s):
                            before = jnp.maximum(s - 1, 0)
                            keep = (row < 3) & (s > 0)
                            there = pl.ds(pl.multiple_of(at_row + s * 16, 16), 16)
                            for c_lo in range(8):
                                c = c_hi * 8 + c_lo
                                lanes = slice(c_lo * LANES, (c_lo + 1) * LANES)
                                at = fh * 48 + kh * 16
                                piece = rbuf[half, s * n_c + c, at : at + 16]
                                if fh == 0:
                                    extra = rbuf[half, before * n_c + c, 32:48]
                                    extra = extra.astype(jnp.float32)[kh * 8 : kh * 8 + 8]
                                    extra = jnp.concatenate(
                                        [
                                            jnp.where(keep, extra, 0.0),
                                            jnp.where(keep, pltpu.roll(extra, 4, 0), 0.0),
                                        ],
                                        axis=0,
                                    )
                                    piece = piece.astype(jnp.float32) + extra
                                xin[there, lanes] = piece.astype(jnp.bfloat16)

                res[fh] = dot(xin[...], ebuf[...])

        for kh in range(2):
            for c_hi in range(2):
                cols = slice(half * 256 + c_hi * LANES, half * 256 + (c_hi + 1) * LANES)
                at_row = (kh * 2 + c_hi) * LANES

                @pl.loop(0, n_s)
                def _(s):
                    low = pl.ds(pl.multiple_of(s * 16, 16), 16)
                    high = pl.ds(pl.multiple_of(128 + s * 16, 16), 16)
                    first = pl.ds(pl.multiple_of(at_row + s * 16, 8), 8)
                    second = pl.ds(pl.multiple_of(at_row + s * 16 + 8, 8), 8)
                    for k8 in range(8):
                        ch = kh * 8 + k8
                        lanes = slice(k8 * LANES, (k8 + 1) * LANES)
                        real = jnp.concatenate([res[0, first, lanes], res[1, first, lanes]], axis=0)
                        imag = jnp.concatenate(
                            [res[0, second, lanes], res[1, second, lanes]], axis=0
                        )
                        xt[ch, low, cols] = real.astype(jnp.bfloat16)
                        xt[ch, high, cols] = imag.astype(jnp.bfloat16)
                        g_re = gains[ch : ch + 1, cols]
                        g_im = gains[16 + ch : 17 + ch, cols]
                        ct[ch, low, cols] = (g_re * real - g_im * imag).astype(jnp.bfloat16)
                        ct[ch, high, cols] = (g_re * imag + g_im * real).astype(jnp.bfloat16)

    for half in range(2):
        for late in range(2):
            sent = sbuf.at[half, pl.ds(0, count - 1), message_rows(half, late)]
            pltpu.make_async_copy(sent, sent, send_sems.at[half, late]).wait()
    sent = table.at[pl.ds(0, 7)]
    pltpu.make_async_copy(sent, sent, steer_sems.at[0]).wait()
    sent = wall.at[pl.ds(0, 4)]
    pltpu.make_async_copy(sent, sent, steer_sems.at[2]).wait()
    sent = wall.at[pl.ds(0, 3)]
    pltpu.make_async_copy(sent, sent, steer_sems.at[5]).wait()


def channelize(voltages, fir_taps, band_start, steer, station_map, beam_index, calib):
    count = lax.axis_size("chan") * lax.axis_size("sect")
    frames = voltages.shape[2] // 4096
    hbm = pl.BlockSpec(memory_space=pl.ANY)
    vmem = pl.BlockSpec(memory_space=pltpu.VMEM)
    half16 = jnp.bfloat16
    return pl.pallas_call(
        spectra_kernel,
        out_shape=(
            pltpu.VMEM((16, 256, 512), half16),
            pltpu.VMEM((16, 256, 512), half16),
            pltpu.VMEM((1024, 512), half16),
            pltpu.VMEM((512, 512), half16),
        ),
        in_specs=[hbm] + [vmem] * 8,
        out_specs=(vmem,) * 4,
        scratch_shapes=[
            pltpu.VMEM((2, frames + 7, 2, HALF, 4096), half16),
            pltpu.VMEM((2, 4, 8, 2, HALF, LANES), jnp.float32),
            pltpu.VMEM((BLOCKS * HALF, 2 * LANES), half16),
            pltpu.VMEM((count * PITCH, LANES), jnp.float32),
            pltpu.VMEM((2, count, ROWS, LANES), half16),
            pltpu.VMEM((2, count, ROWS, LANES), half16),
            pltpu.VMEM((512, 1024), half16),
            pltpu.VMEM((2, 512, 1024), jnp.float32),
            pltpu.VMEM((1024, 1024), half16),
            pltpu.VMEM((32, 512), jnp.float32),
            pltpu.VMEM((8, LANES, LANES), half16),
            pltpu.VMEM((512, LANES), half16),
            pltpu.VMEM((8, 512, LANES), half16),
            pltpu.VMEM((LANES, 2 * LANES), half16),
            pltpu.VMEM((1, 512), jnp.int32),
            pltpu.VMEM((512, 1024), half16),
            pltpu.VMEM((8, LANES, LANES), half16),
            pltpu.SemaphoreType.DMA((2, 2)),
            pltpu.SemaphoreType.DMA((2, 2)),
            pltpu.SemaphoreType.DMA((2, 2)),
            pltpu.SemaphoreType.DMA((6,)),
        ],
        compiler_params=pltpu.CompilerParams(
            collective_id=0, has_side_effects=True, vmem_limit_bytes=48 * 1024 * 1024
        ),
        name="spectra",
    )(
        voltages,
        steer,
        fir_taps,
        jnp.asarray(twiddles()),
        jnp.asarray(lane_table()),
        band_start.reshape(1, 32),
        station_map.reshape(1, 512),
        beam_index.reshape(1, -1),
        calib.reshape(32, 512),
    )


def product_kernel(
    scale, xt, ct, weights, order, vis, beams, zbuf, wbuf, bbuf, obuf, pbuf, beam_sems, vis_sems
):
    n_b = beams.shape[1]
    tiles = bbuf.shape[0]

    @pl.loop(0, xt.shape[0], unroll=8)
    def _(ch):
        uv = dot(weights[...], ct[ch], NT)
        real = uv[:512, :128] - uv[512:, 128:]
        imag = uv[:512, 128:] + uv[512:, :128]
        both = jnp.concatenate([real, imag], axis=1).astype(jnp.bfloat16)
        rows = pl.ds(pl.multiple_of(ch * 16, 16), 16)
        bbuf[:, rows, :] = both.reshape(tiles, 16, 256)

    line = iota((256, 256), 0)
    source = lax.rem(line, 16) * 16 + line // 16
    move = one_hot(iota((256, 256), 1) == source)

    @pl.loop(0, tiles // 4, unroll=4)
    def _(four):
        for j in range(4):
            tile = four * 4 + j
            out = dot(move, bbuf[tile]).astype(jnp.bfloat16)
            for part in range(2):
                piece = out[:, part * 128 : (part + 1) * 128].reshape(16, 16, 128)
                obuf[part, pl.ds(tile * 16, 16)] = piece

    def put_beams(part):
        return pltpu.make_async_copy(
            obuf.at[part, pl.ds(0, n_b)], beams.at[part], beam_sems.at[part]
        )

    def put_vis(part, g):
        return pltpu.make_async_copy(pbuf.at[part, g % 2], vis.at[part, g], vis_sems.at[part, g % 2])

    for part in range(2):
        put_beams(part).start()

    for g in range(4):
        for a in range(4):
            z = dot(order[...], xt[g * 4 + a], NT).astype(jnp.bfloat16)
            zbuf[:, a * 256 : (a + 1) * 256] = z
            wbuf[:, a * 256 : a * 256 + 128] = z[:, 128:]
            wbuf[:, a * 256 + 128 : (a + 1) * 256] = -z[:, :128]
        for part, left in enumerate((zbuf, wbuf)):
            if g >= 2:
                put_vis(part, g - 2).wait()
            pbuf[part, g % 2] = dot(left[...], zbuf[...], NT) * scale
            put_vis(part, g).start()

    for part in range(2):
        for g in (2, 3):
            put_vis(part, g).wait()
        put_beams(part).wait()


def products(xt, ct, weights, order):
    half16 = jnp.bfloat16
    hbm = pl.BlockSpec(memory_space=pl.ANY)
    vmem = pl.BlockSpec(memory_space=pltpu.VMEM)
    vis, beams = pl.pallas_call(
        functools.partial(product_kernel, 1.0 / 512.0),
        out_shape=(
            jax.ShapeDtypeStruct((2, 4, 512, 512), jnp.float32),
            jax.ShapeDtypeStruct((2, 500, 16, 128), half16),
        ),
        in_specs=[vmem] * 4,
        out_specs=(hbm, hbm),
        scratch_shapes=[
            pltpu.VMEM((512, 1024), half16),
            pltpu.VMEM((512, 1024), half16),
            pltpu.VMEM((32, 256, 256), half16),
            pltpu.VMEM((2, 512, 16, 128), half16),
            pltpu.VMEM((2, 2, 512, 512), jnp.float32),
            pltpu.SemaphoreType.DMA((2,)),
            pltpu.SemaphoreType.DMA((2, 2)),
        ],
        compiler_params=pltpu.CompilerParams(vmem_limit_bytes=40 * 1024 * 1024),
        name="products",
    )(xt, ct, weights, order)
    return vis, jnp.transpose(beams, (0, 2, 1, 3))


def shards(voltages, fir_taps, station_map, band_start, calib, steer, beam_index):
    parts = channelize(
        voltages, fir_taps, band_start, steer, station_map, beam_index, calib
    )
    return products(*parts)


def solution(mesh):
    return jax.shard_map(
        shards,
        mesh=mesh,
        in_specs=(
            P(None, "chan", "sect"),
            P(),
            P(),
            P(),
            P(None, ("chan", "sect"), None),
            P("sect", None, None),
            P(),
        ),
        out_specs=(P(None, ("chan", "sect"), None, None), P(None, ("chan", "sect"), None, None)),
        check_vma=False,
    )
```
